32 devices in a mesh: doc: 4 (over y, core), seq: 8 (over z, x).
Axes of the slice: x: 2, y: 2, z: 4, core: 2. Of those that a mesh axis runs over, the one named last changes fastest.
Arguments:
- hidden: bfloat16 [4, 4096, 768], P('doc', 'seq'), may hold values from -6 to 6
- token_ids: int32 [4, 4096], P('doc', 'seq'), may hold values from 0 to 50264, as said below
- w_query: bfloat16 [768, 768], replicated, may hold values from -0.625 to 0.625
- w_keyval: bfloat16 [768, 1536], replicated, may hold values from -0.21875 to 0.21875
- w_out: bfloat16 [768, 768], replicated, may hold values from -0.21875 to 0.21875
- x_query: bfloat16 [768, 768], replicated, may hold values from -0.21875 to 0.21875
- x_out: bfloat16 [768, 768], replicated, may hold values from -0.21875 to 0.21875
- shortlist: int32 [4, 320], P('doc'), may hold values from 0 to 9215, as said below
- code_row: int32 [9216], replicated, may hold values from 0 to 9215, as said below
- code_cache: bfloat16 [9216, 2, 8, 768], P(('doc', 'seq')), may hold values from -10 to 10
Outputs:
- refined: bfloat16 [4, 4096, 768], P('doc', 'seq')
- cand_score: float32 [4, 320], P('doc')
The draws below stay inside these ranges and needn't reach their ends.
Inputs may be any that keep to these rules, and one draw needn't show every extreme that they name: `token_ids`: each summary is a run of ids of 1 or more followed by padding ids 0 up to its end; every summary has 1024 or more nonzero ids and one summary has no padding. `shortlist`: the candidates of one summary are distinct codes; at most 16 of them have code_row in one block of 288 rows (row // 288 equal), and for every summary some block holds exactly 16 of them. `code_row`: each row of the cache holds exactly one code.
All inputs are finite; a program needn't handle non-finite values.
Results may differ from the reference program's by a relative error of at most 0.018.
Values may be sent and summed in bfloat16 or wider, within the bound.
A program may use at most 192 MiB of HBM per device.

```python
import math
import jax
import jax.numpy as jnp
from jax import lax

D = 768
HEADS = 12
HALF_WIN = 256
TOK_DEV = 512
SEQ_LEN = 4096
DOCS = 4
C = 320
DESC = 8
CODE_DEV = 288
CODES = 9216
CAP = 16
VOCAB = 50265
DEVICES = 32


def code_layout(key):
    return jax.random.permutation(jax.random.fold_in(key, 701), CODES).astype(jnp.int32)


def draw_code_row(key, part):
    return code_layout(key)


def draw_shortlist(key, part):
    layout = code_layout(key)
    code_of_row = jnp.zeros((CODES,), jnp.int32).at[layout].set(jnp.arange(CODES, dtype=jnp.int32))
    grid_size = DEVICES * CAP
    owner_ids = jnp.arange(DEVICES, dtype=jnp.int32)
    popular = jax.random.randint(jax.random.fold_in(key, 711), (DEVICES,), 0, 4)
    noise = jax.random.randint(jax.random.fold_in(key, 712), (DOCS, DEVICES, CAP), 0, 65536)
    full_owner = jax.random.randint(jax.random.fold_in(key, 713), (DOCS,), 0, DEVICES)
    boost = popular[None, :] + 8 * (owner_ids[None, :] == full_owner[:, None]).astype(jnp.int32)
    position = jnp.arange(grid_size, dtype=jnp.int32).reshape(DEVICES, CAP)
    scores = (boost[:, :, None] * 65536 + noise) * grid_size + position[None]
    unused, picked = lax.top_k(scores.reshape(DOCS, grid_size), C)
    picked = picked.astype(jnp.int32)
    owner_dev = picked // CAP
    slot_rank = picked % CAP
    offsets = jax.random.randint(jax.random.fold_in(key, 714), (DOCS, DEVICES), 0, CODE_DEV)
    local_row = (jnp.take_along_axis(offsets, owner_dev, axis=1) + slot_rank) % CODE_DEV
    return code_of_row[owner_dev * CODE_DEV + local_row]


def draw_token_ids(key, part):
    lengths = jax.random.randint(jax.random.fold_in(key, 721), (DOCS,), SEQ_LEN // 4, SEQ_LEN + 1)
    full_doc = jax.random.randint(jax.random.fold_in(key, 722), (), 0, DOCS)
    doc_ids = jnp.arange(DOCS)
    lengths = jnp.where(doc_ids == full_doc, SEQ_LEN, lengths)
    words = jax.random.randint(jax.random.fold_in(key, 723), (DOCS, SEQ_LEN), 1, VOCAB)
    positions = jnp.arange(SEQ_LEN)[None, :]
    top_spot = (doc_ids[:, None] == full_doc) & (positions == 0)
    words = jnp.where(top_spot, VOCAB - 1, words)
    return jnp.where(positions < lengths[:, None], words, 0).astype(jnp.int32)


def steps_of(key, extent, pieces, least, high):
    def one(dim, blocks):
        heights = jax.random.uniform(jax.random.fold_in(jax.random.fold_in(key, 6), dim), (blocks,), jnp.float32, least / len(pieces), high / len(pieces))
        return jnp.repeat(jnp.exp(heights), extent[dim] // blocks).reshape((-1,) + (1,) * (len(extent) - dim - 1))

    loudness = one(*pieces[0])
    for cut in pieces[1:]:
        loudness = loudness * one(*cut)
    return loudness


def normal_values(rng, shape, scale, most, shards=(), held_as=jnp.bfloat16):
    gain = steps_of(rng, shape, shards, -0.22, 0.18) if shards else 1.0
    entries = jax.random.normal(rng, shape, jnp.float32) * scale * gain
    return jnp.minimum(jnp.maximum(entries, -most), most).astype(held_as)


def setup_inputs(seed: int = 0) -> dict:
    seeds = jax.random.split(jax.random.key(seed), 11)
    hidden = normal_values(seeds[0], (DOCS, SEQ_LEN, D), 1.0, 6.0, ((0, 4), (1, 8)))
    token_ids = draw_token_ids(jax.random.fold_in(seeds[10], 71), 0)
    w_query = normal_values(seeds[2], (D, D), (D // 8) ** -0.5, 0.625)
    w_keyval = normal_values(seeds[3], (D, 2 * D), D ** -0.5, 0.21875)
    w_out = normal_values(seeds[4], (D, D), D ** -0.5, 0.21875)
    x_query = normal_values(seeds[5], (D, D), D ** -0.5, 0.21875)
    x_out = normal_values(seeds[6], (D, D), D ** -0.5, 0.21875)
    shortlist = draw_shortlist(jax.random.fold_in(seeds[10], 71), 0)
    code_row = draw_code_row(jax.random.fold_in(seeds[10], 71), 0)
    code_cache = normal_values(seeds[9], (CODES, 2, DESC, D), 2.0, 10.0, ((0, 32),))
    return {"hidden": hidden, "token_ids": token_ids, "w_query": w_query, "w_keyval": w_keyval, "w_out": w_out, "x_query": x_query, "x_out": x_out, "shortlist": shortlist, "code_row": code_row, "code_cache": code_cache}


def layer_norm(values):
    centered = values - lax.optimization_barrier(jnp.mean(values, axis=-1, keepdims=True))
    spread = lax.optimization_barrier(jnp.mean(centered * centered, axis=-1, keepdims=True))
    return centered * lax.rsqrt(spread + 1e-05)

def attend(query, key_rows, value_rows, allowed, weigh):
    query_count = query.shape[0]
    key_count = key_rows.shape[0]
    head_size = query.shape[1] // HEADS
    score_scale = 1.0 / math.sqrt(head_size)
    query_heads = lax.optimization_barrier(query).astype(jnp.float32).reshape(query_count, HEADS, head_size)
    key_heads = lax.optimization_barrier(key_rows).astype(jnp.float32).reshape(key_count, HEADS, head_size)
    value_heads = lax.optimization_barrier(value_rows).astype(jnp.float32).reshape(key_count, HEADS, head_size)
    scores = jnp.einsum('qhd,khd->hqk', query_heads, key_heads) * score_scale
    expd = jnp.exp(scores)
    if allowed is not None:
        expd = jnp.where(allowed[None], expd, 0.0)
    weights = expd / lax.optimization_barrier(jnp.sum(expd, axis=-1, keepdims=True))
    probs = lax.optimization_barrier(weights.astype(jnp.bfloat16)).astype(jnp.float32)
    context = jnp.einsum('hqk,khd->qhd', probs, value_heads).reshape(query_count, HEADS * head_size)
    context = context.astype(jnp.bfloat16)
    if weigh is None:
        return (context, None)
    key_mass = lax.optimization_barrier(jnp.sum(jnp.where(weigh[None, :, None], weights, 0.0), axis=(0, 1)))
    return (context, key_mass)

def reference(hidden, token_ids, w_query, w_keyval, w_out, x_query, x_out, shortlist, code_row, code_cache):
    block_count = SEQ_LEN // TOK_DEV

    def one_document(operands):
        doc_hidden, doc_tokens, doc_shortlist = operands
        length = jnp.sum((doc_tokens != 0).astype(jnp.int32))
        normed = layer_norm(doc_hidden.astype(jnp.float32)).astype(jnp.bfloat16)
        query = jnp.dot(normed, w_query, preferred_element_type=jnp.float32).astype(jnp.bfloat16)
        keyval = jnp.dot(normed, w_keyval, preferred_element_type=jnp.float32).astype(jnp.bfloat16)
        padded = jnp.pad(keyval, ((HALF_WIN, HALF_WIN), (0, 0)))

        def window_block(block_index):
            first_row = (block_index * TOK_DEV).astype(jnp.int32)
            block_query = lax.dynamic_slice_in_dim(query, first_row, TOK_DEV, 0)
            block_keys = lax.dynamic_slice_in_dim(padded, first_row, TOK_DEV + 2 * HALF_WIN, 0)
            query_pos = first_row + jnp.arange(TOK_DEV, dtype=jnp.int32)
            key_pos = first_row - HALF_WIN + jnp.arange(TOK_DEV + 2 * HALF_WIN, dtype=jnp.int32)
            near = jnp.abs(query_pos[:, None] - key_pos[None, :]) <= HALF_WIN
            usable = ((key_pos >= 0) & (key_pos < length))[None, :] | (query_pos[:, None] == key_pos[None, :])
            context, unused = attend(block_query, block_keys[:, :D], block_keys[:, D:], near & usable, None)
            return context
        contexts = lax.map(window_block, jnp.arange(block_count, dtype=jnp.int32))
        context = contexts.reshape(SEQ_LEN, D)
        middle = (doc_hidden.astype(jnp.float32) + jnp.dot(context, w_out, preferred_element_type=jnp.float32)).astype(jnp.bfloat16)
        middle_wide = lax.optimization_barrier(middle).astype(jnp.float32)
        cross_normed = layer_norm(middle_wide).astype(jnp.bfloat16)
        cross_query = jnp.dot(cross_normed, x_query, preferred_element_type=jnp.float32).astype(jnp.bfloat16)
        cache_rows = code_cache[code_row[doc_shortlist]]
        cand_keys = cache_rows[:, 0].reshape(C * DESC, D)
        cand_values = cache_rows[:, 1].reshape(C * DESC, D)

        def cross_block(block_index):
            first_row = (block_index * TOK_DEV).astype(jnp.int32)
            block_query = lax.dynamic_slice_in_dim(cross_query, first_row, TOK_DEV, 0)
            query_pos = first_row + jnp.arange(TOK_DEV, dtype=jnp.int32)
            return attend(block_query, cand_keys, cand_values, None, query_pos < length)
        cross_contexts, masses = lax.map(cross_block, jnp.arange(block_count, dtype=jnp.int32))
        cross_context = cross_contexts.reshape(SEQ_LEN, D)
        refined = (middle_wide + jnp.dot(cross_context, x_out, preferred_element_type=jnp.float32)).astype(jnp.bfloat16)
        cand_mass = lax.optimization_barrier(jnp.sum(lax.optimization_barrier(jnp.sum(masses, axis=0)).reshape(C, DESC), axis=1))
        cand_score = C * cand_mass / (HEADS * length.astype(jnp.float32))
        return (refined, cand_score)
    return lax.map(one_document, (hidden, token_ids, shortlist))
```

```python
import functools
import math

import jax
import jax.numpy as jnp
from jax import lax
from jax.experimental import pallas as pl
from jax.experimental.pallas import tpu as pltpu
from jax.sharding import PartitionSpec as P

HEADS = 12
HEAD = 64
HALF_WIN = 256
DESC = 8
GROUPS = 4
EXP2_SCALE = math.log2(math.e) / math.sqrt(HEAD)
F32 = jnp.float32
BF16 = jnp.bfloat16
NT = (((1,), (1,)), ((), ()))


def layer_norm(values):
    centered = values - jnp.mean(values, axis=-1, keepdims=True)
    spread = jnp.mean(centered * centered, axis=-1, keepdims=True)
    return centered * lax.rsqrt(spread + 1e-05)


def window_kernel(valid_ref, q_ref, kl_ref, ko_ref, kh_ref, vl_ref, vo_ref, vh_ref, o_ref, bias):
    rows = q_ref.shape[0]
    half = HALF_WIN
    blocks = rows // half
    width = 3 * half

    @pl.when(pl.program_id(0) == 0)
    def _():
        for b in range(blocks):
            i = lax.broadcasted_iota(jnp.int32, (half, width), 0)
            j = lax.broadcasted_iota(jnp.int32, (half, width), 1)
            ok = valid_ref[:, b * half : b * half + width] > 0.0
            allowed = (j >= i) & (j <= i + 2 * half) & (ok | (j == i + half))
            bias[b] = jnp.where(allowed, 0.0, -1e30)

    k = jnp.concatenate([kl_ref[...], ko_ref[...], kh_ref[...]], axis=0)
    v = jnp.concatenate([vl_ref[...], vo_ref[...], vh_ref[...]], axis=0)
    v = jnp.concatenate([v, jnp.ones_like(v)], axis=1)
    lane = lax.broadcasted_iota(jnp.int32, (half, 2 * HEAD), 1)
    for b in range(blocks):
        q = q_ref[b * half : (b + 1) * half, :]
        kb = k[b * half : b * half + width]
        vb = v[b * half : b * half + width]
        outs = []
        for h in range(2):
            mine = (lane >= h * HEAD) & (lane < (h + 1) * HEAD)
            s = lax.dot_general(
                jnp.where(mine, q, jnp.zeros_like(q)), kb, NT, preferred_element_type=F32
            )
            e = jnp.exp2(s * EXP2_SCALE + bias[b])
            o = jnp.dot(e.astype(BF16), vb, preferred_element_type=F32)
            outs.append(o[:, : 2 * HEAD] / o[:, 2 * HEAD :])
        o_ref[b * half : (b + 1) * half, :] = jnp.where(lane < HEAD, outs[0], outs[1]).astype(BF16)


def window_attend(valid, query, low, own, high):
    rows, width = query.shape
    pairs = width // (2 * HEAD)
    span = rows + 2 * HALF_WIN

    def cols(r, first):
        return pl.BlockSpec((r, 2 * HEAD), lambda p: (0, p + first))

    return pl.pallas_call(
        window_kernel,
        grid=(pairs,),
        out_shape=jax.ShapeDtypeStruct((rows, width), BF16),
        in_specs=[
            pl.BlockSpec((1, span), lambda p: (0, 0)),
            cols(rows, 0),
            cols(HALF_WIN, 0),
            cols(rows, 0),
            cols(HALF_WIN, 0),
            cols(HALF_WIN, pairs),
            cols(rows, pairs),
            cols(HALF_WIN, pairs),
        ],
        out_specs=cols(rows, 0),
        scratch_shapes=[pltpu.VMEM((rows // HALF_WIN, HALF_WIN, 3 * HALF_WIN), F32)],
        compiler_params=pltpu.CompilerParams(vmem_limit_bytes=48 * 1024 * 1024),
        cost_estimate=pl.CostEstimate(
            flops=8 * rows * 3 * HALF_WIN * width,
            bytes_accessed=8 * rows * width,
            transcendentals=rows * 3 * HALF_WIN * HEADS,
        ),
    )(valid, query, low, own, high, low, own, high)


def cross_kernel(chunk, weigh_ref, q_ref, k_ref, v_ref, o_ref, mass_ref):
    tile = q_ref.shape[0]
    keys, wide = k_ref.shape
    heads = (wide - HEAD) // HEAD
    lane = lax.broadcasted_iota(jnp.int32, (tile, wide), 1)
    q = q_ref[...]
    q = jnp.concatenate([jnp.zeros((tile, HEAD), BF16), q], axis=1)

    @pl.when(pl.program_id(0) == 0)
    def _():
        mass_ref[...] = jnp.zeros_like(mass_ref)

    context = jnp.zeros((tile, wide), F32)
    for h in range(heads):
        qh = jnp.where((lane >= (h + 1) * HEAD) & (lane < (h + 2) * HEAD), q, jnp.zeros_like(q))
        parts = []
        o = jnp.zeros((tile, wide), F32)
        for c in range(0, keys, chunk):
            s = lax.dot_general(qh, k_ref[c : c + chunk, :], NT, preferred_element_type=F32)
            e = jnp.exp2(s * EXP2_SCALE)
            o += jnp.dot(e.astype(BF16), v_ref[c : c + chunk, :], preferred_element_type=F32)
            parts.append(e)
        inverse = 1.0 / o[:, heads * HEAD : heads * HEAD + 1]
        context = jnp.where((lane >= h * HEAD) & (lane < (h + 1) * HEAD), o * inverse, context)
        weight = inverse * weigh_ref[...]
        for c, e in zip(range(0, keys, chunk), parts):
            mass_ref[:, c : c + chunk] += jnp.sum(
                (e * weight).reshape(tile // 8, 8, chunk), axis=0
            )
    o_ref[...] = context[:, : heads * HEAD].astype(BF16)


def cross_attend(weigh, query, key_rows, value_rows):
    rows, width = query.shape
    keys, wide = key_rows.shape
    tile = 256
    return pl.pallas_call(
        functools.partial(cross_kernel, 512),
        grid=(rows // tile,),
        out_shape=(
            jax.ShapeDtypeStruct((rows, width), BF16),
            jax.ShapeDtypeStruct((8, keys), F32),
        ),
        in_specs=[
            pl.BlockSpec((tile, 1), lambda i: (i, 0)),
            pl.BlockSpec((tile, width), lambda i: (i, 0)),
            pl.BlockSpec((keys, wide), lambda i: (0, 0)),
            pl.BlockSpec((keys, wide), lambda i: (0, 0)),
        ],
        out_specs=(
            pl.BlockSpec((tile, width), lambda i: (i, 0)),
            pl.BlockSpec((8, keys), lambda i: (0, 0)),
        ),
        compiler_params=pltpu.CompilerParams(vmem_limit_bytes=48 * 1024 * 1024),
        cost_estimate=pl.CostEstimate(
            flops=16 * rows * keys * width,
            bytes_accessed=4 * keys * wide + 4 * rows * width,
            transcendentals=3 * rows * keys,
        ),
    )(weigh, query, key_rows, value_rows)


def local(
    hidden, token_ids, w_query, w_keyval, w_out, x_query, x_out, shortlist, code_row, code_cache
):
    doc_hidden = hidden[0]
    doc_tokens = token_ids[0]
    tok_rows, width = doc_hidden.shape
    seq_count = lax.axis_size("seq")
    doc_count = lax.axis_size("doc")
    devices = seq_count * doc_count
    across = seq_count // GROUPS
    seq_index = lax.axis_index("seq")
    doc_index = lax.axis_index("doc")
    me = doc_index * seq_count + seq_index
    group = seq_index // across
    cand_count = shortlist.shape[1]
    code_dev = code_cache.shape[0]
    capacity = 8 * cand_count // (5 * devices)
    slots = devices * capacity
    part = width // GROUPS

    cache_rows = code_row[shortlist[0]]
    relative = [cache_rows]
    for r in range(1, doc_count):
        relative.append(
            lax.ppermute(cache_rows, "doc", [(i, (i + r) % doc_count) for i in range(doc_count)])
        )
    relative = jnp.stack(relative)
    docs = jnp.arange(doc_count, dtype=jnp.int32)
    source = (doc_index - docs) % doc_count
    rows_of = jnp.sum(
        jnp.where((source[None, :] == docs[:, None])[:, :, None], relative[None], 0), axis=1
    )
    order = jnp.arange(cand_count, dtype=jnp.int32)
    before = (order[:, None] < order[None, :]).astype(BF16)
    held = rows_of // code_dev == me
    rank = jnp.dot(held.astype(BF16), before, preferred_element_type=F32).astype(jnp.int32)
    slot = jnp.arange(capacity, dtype=jnp.int32)
    request = jnp.sum(
        jnp.where(
            held[:, None, :] & (rank[:, None, :] == slot[None, :, None]),
            (rows_of % code_dev)[:, None, :],
            0,
        ),
        axis=2,
    )
    picked = code_cache[request.reshape(-1)]
    picked = picked.reshape(doc_count, capacity, 2, across, DESC // across, GROUPS, part)
    picked = jnp.flip(picked, axis=2).transpose(0, 5, 3, 4, 1, 2, 6)
    picked = picked.reshape(devices, DESC // across, capacity, 2 * part)
    arrived = lax.all_to_all(picked, ("doc", "seq"), split_axis=0, concat_axis=0, tiled=True)

    owner = cache_rows // code_dev
    onehot = (owner[:, None] == jnp.arange(devices, dtype=jnp.int32)[None, :]).astype(BF16)
    ahead = jnp.dot(before.T, onehot, preferred_element_type=F32)
    slot_rank = jnp.sum(ahead * onehot, axis=1).astype(jnp.int32)
    slot_index = owner * capacity + slot_rank
    choose = (slot_index[:, None] == jnp.arange(slots, dtype=jnp.int32)[None, :]).astype(BF16)

    normed = layer_norm(doc_hidden.astype(F32)).astype(BF16)
    query = jnp.dot(normed, w_query, preferred_element_type=F32).astype(BF16)
    keyval = jnp.dot(normed, w_keyval, preferred_element_type=F32).astype(BF16)
    up = [(i, i + 1) for i in range(seq_count - 1)]
    down = [(i + 1, i) for i in range(seq_count - 1)]
    live = (doc_tokens != 0).astype(F32)
    low_live = lax.ppermute(live[tok_rows - HALF_WIN :], "seq", up)
    high_live = lax.ppermute(live[:HALF_WIN], "seq", down)
    low = lax.ppermute(keyval[tok_rows - HALF_WIN :], "seq", up)
    high = lax.ppermute(keyval[:HALF_WIN], "seq", down)
    length = lax.psum(jnp.sum((doc_tokens != 0).astype(jnp.int32)), "seq")
    valid = jnp.concatenate([low_live, live, high_live])[None]
    context = window_attend(valid, query, low, keyval, high)
    middle = (
        doc_hidden.astype(F32) + jnp.dot(context, w_out, preferred_element_type=F32)
    ).astype(BF16)
    middle_wide = middle.astype(F32)
    cross_normed = layer_norm(middle_wide).astype(BF16)
    cross_query = jnp.dot(cross_normed, x_query, preferred_element_type=F32).astype(BF16)

    def turn(r):
        return [
            (i, (i // across + r) % GROUPS * across + i % across) for i in range(seq_count)
        ]

    def piece(array, g):
        return lax.dynamic_slice_in_dim(array, g * part, part, axis=1)

    queries = [piece(cross_query, group)]
    for r in range(1, GROUPS):
        queries.append(
            lax.ppermute(piece(cross_query, (group + r) % GROUPS), "seq", turn(r))
        )

    arrived = arrived.transpose(1, 0, 2, 3).reshape(DESC // across, slots, 2 * part)
    own_rows = jnp.einsum("cs,tsf->tcf", choose, arrived, preferred_element_type=F32).astype(BF16)
    own_rows = own_rows.reshape(DESC // across * cand_count, 2 * part)
    all_rows = [own_rows]
    for r in range(1, across):
        step = [(i, i // across * across + (i % across + r) % across) for i in range(seq_count)]
        all_rows.append(lax.ppermute(own_rows, "seq", step))
    all_rows = jnp.concatenate(all_rows)
    column = jnp.arange(part + HEAD)
    value_rows = jnp.where(
        column[None, :] < part, all_rows[:, : part + HEAD], jnp.ones((), BF16)
    )
    key_rows = all_rows[:, part - HEAD :]

    mass = 0.0
    returned = [None] * GROUPS
    for r in (2, 1, 3, 0):
        origin = (group - r) % GROUPS * across + seq_index % across
        position = origin * tok_rows + jnp.arange(tok_rows, dtype=jnp.int32)
        weigh = (position < length).astype(F32)[:, None]
        piece_context, piece_mass = cross_attend(weigh, queries[r], key_rows, value_rows)
        mass = mass + piece_mass
        returned[r] = (
            lax.ppermute(piece_context, "seq", turn(GROUPS - r)) if r else piece_context
        )
    total = middle_wide
    for r in range(GROUPS):
        rows = lax.dynamic_slice_in_dim(x_out, (group + r) % GROUPS * part, part, axis=0)
        total = total + jnp.dot(returned[r], rows, preferred_element_type=F32)
    refined = total.astype(BF16)
    local_mass = jnp.sum(mass.reshape(8, DESC, cand_count), axis=(0, 1))
    cand_mass = lax.psum(local_mass, "seq")
    cand_score = cand_count * cand_mass / (HEADS * length.astype(F32))
    return (refined[None], cand_score[None])


def solution(mesh):
    return jax.shard_map(
        local,
        mesh=mesh,
        in_specs=(
            P("doc", "seq", None),
            P("doc", "seq"),
            P(),
            P(),
            P(),
            P(),
            P(),
            P("doc", None),
            P(),
            P(("doc", "seq"), None, None, None),
        ),
        out_specs=(P("doc", "seq", None), P("doc", None)),
        check_vma=False,
    )
```

```python
import functools
import math

import jax
import jax.numpy as jnp
from jax import lax
from jax.experimental import pallas as pl
from jax.experimental.pallas import tpu as pltpu
from jax.sharding import PartitionSpec as P

HEADS = 12
HEAD = 64
HALF_WIN = 256
DESC = 8
GROUPS = 4
EXP2_SCALE = math.log2(math.e) / math.sqrt(HEAD)
F32 = jnp.float32
BF16 = jnp.bfloat16
NT = (((1,), (1,)), ((), ()))


def layer_norm(values):
    centered = values - jnp.mean(values, axis=-1, keepdims=True)
    spread = jnp.mean(centered * centered, axis=-1, keepdims=True)
    return centered * lax.rsqrt(spread + 1e-05)


def window_kernel(valid_ref, q_ref, kl_ref, ko_ref, kh_ref, vl_ref, vo_ref, vh_ref, o_ref, bias):
    rows = q_ref.shape[0]
    half = HALF_WIN
    blocks = rows // half
    width = 3 * half

    @pl.when(pl.program_id(0) == 0)
    def _():
        for b in range(blocks):
            i = lax.broadcasted_iota(jnp.int32, (half, width), 0)
            j = lax.broadcasted_iota(jnp.int32, (half, width), 1)
            ok = valid_ref[:, b * half : b * half + width] > 0.0
            allowed = (j >= i) & (j <= i + 2 * half) & (ok | (j == i + half))
            bias[b] = jnp.where(allowed, 0.0, -1e30)

    k = jnp.concatenate([kl_ref[...], ko_ref[...], kh_ref[...]], axis=0)
    v = jnp.concatenate([vl_ref[...], vo_ref[...], vh_ref[...]], axis=0)
    v = jnp.concatenate([v, jnp.ones_like(v)], axis=1)
    lane = lax.broadcasted_iota(jnp.int32, (half, 2 * HEAD), 1)
    for b in range(blocks):
        q = q_ref[b * half : (b + 1) * half, :]
        kb = k[b * half : b * half + width]
        vb = v[b * half : b * half + width]
        outs = []
        for h in range(2):
            mine = (lane >= h * HEAD) & (lane < (h + 1) * HEAD)
            s = lax.dot_general(
                jnp.where(mine, q, jnp.zeros_like(q)), kb, NT, preferred_element_type=F32
            )
            e = jnp.exp2(s * EXP2_SCALE + bias[b])
            o = jnp.dot(e.astype(BF16), vb, preferred_element_type=F32)
            outs.append(o[:, : 2 * HEAD] / o[:, 2 * HEAD :])
        o_ref[b * half : (b + 1) * half, :] = jnp.where(lane < HEAD, outs[0], outs[1]).astype(BF16)


def window_attend(valid, query, low, own, high):
    rows, width = query.shape
    pairs = width // (2 * HEAD)
    span = rows + 2 * HALF_WIN

    def cols(r, first):
        return pl.BlockSpec((r, 2 * HEAD), lambda p: (0, p + first))

    return pl.pallas_call(
        window_kernel,
        grid=(pairs,),
        out_shape=jax.ShapeDtypeStruct((rows, width), BF16),
        in_specs=[
            pl.BlockSpec((1, span), lambda p: (0, 0)),
            cols(rows, 0),
            cols(HALF_WIN, 0),
            cols(rows, 0),
            cols(HALF_WIN, 0),
            cols(HALF_WIN, pairs),
            cols(rows, pairs),
            cols(HALF_WIN, pairs),
        ],
        out_specs=cols(rows, 0),
        scratch_shapes=[pltpu.VMEM((rows // HALF_WIN, HALF_WIN, 3 * HALF_WIN), F32)],
        compiler_params=pltpu.CompilerParams(vmem_limit_bytes=48 * 1024 * 1024),
        cost_estimate=pl.CostEstimate(
            flops=8 * rows * 3 * HALF_WIN * width,
            bytes_accessed=8 * rows * width,
            transcendentals=rows * 3 * HALF_WIN * HEADS,
        ),
    )(valid, query, low, own, high, low, own, high)


def gather_kernel(docs, capacity, request_ref, cache_ref, order_ref, out_ref, held, sems):
    count = docs * capacity
    step = 2 * DESC
    part = out_ref.shape[-1] // 2

    def fetch(i):
        row = pl.multiple_of(request_ref[i] * step, step)
        return pltpu.make_async_copy(
            cache_ref.at[pl.ds(row, step)], held.at[pl.ds(i * step, step)], sems.at[i]
        )

    for i in range(count):
        fetch(i).start()
    rows = capacity * step
    half = capacity * DESC
    for d in range(docs):
        for i in range(d * capacity, (d + 1) * capacity):
            fetch(i).wait()
        ordered = jnp.dot(
            order_ref[...], held[d * rows : (d + 1) * rows, :], preferred_element_type=F32
        ).astype(BF16)
        for g in range(GROUPS):
            cols = slice(g * part, (g + 1) * part)
            out_ref[d, g] = jnp.concatenate([ordered[:half, cols], ordered[half:, cols]], axis=1)


def gather_rows(request, cache, capacity):
    docs = request.shape[0] // capacity
    codes, pair, desc, width = cache.shape
    part = width // GROUPS
    rows = capacity * pair * desc
    out = jnp.arange(rows)
    source = out % capacity * (2 * desc) + (1 - out // (desc * capacity)) * desc
    source = source + out // capacity % desc
    order = (source[:, None] == out[None, :]).astype(BF16)
    return pl.pallas_call(
        functools.partial(gather_kernel, docs, capacity),
        out_shape=jax.ShapeDtypeStruct((docs, GROUPS, rows // 2, 2 * part), BF16),
        in_specs=[
            pl.BlockSpec(memory_space=pltpu.SMEM),
            pl.BlockSpec(memory_space=pl.ANY),
            pl.BlockSpec(memory_space=pltpu.VMEM),
        ],
        out_specs=pl.BlockSpec(memory_space=pltpu.VMEM),
        scratch_shapes=[
            pltpu.VMEM((docs * rows, width), BF16),
            pltpu.SemaphoreType.DMA((docs * capacity,)),
        ],
        compiler_params=pltpu.CompilerParams(vmem_limit_bytes=48 * 1024 * 1024),
        cost_estimate=pl.CostEstimate(
            flops=2 * docs * rows * rows * width,
            bytes_accessed=4 * docs * rows * width,
            transcendentals=0,
        ),
    )(request, cache.reshape(codes * pair * desc, width), order)


def cross_kernel(
    seq_count,
    chunk,
    count_ref,
    q_ref,
    k_ref,
    v_ref,
    middle_ref,
    w_ref,
    o_ref,
    mass_ref,
    context,
    landed,
    mass,
    masses,
    send_sem,
    recv_sem,
    mass_send,
    mass_recv,
):
    me = lax.axis_index("seq")
    across = seq_count // GROUPS
    group = me // across
    column = me % across
    keys, wide = k_ref.shape
    tile = 256
    tiles = q_ref.shape[1] // tile
    part = wide - HEAD
    heads = part // HEAD
    lane = lax.broadcasted_iota(jnp.int32, (tile, wide), 1)

    barrier = pltpu.get_barrier_semaphore()
    for p in range(1, seq_count):
        pl.semaphore_signal(
            barrier,
            inc=1,
            device_id={"seq": (me + p) % seq_count},
            device_id_type=pl.DeviceIdType.MESH,
        )
    mass[...] = jnp.zeros_like(mass)

    def send_back(r):
        return pltpu.make_async_remote_copy(
            src_ref=context.at[r],
            dst_ref=landed.at[r],
            send_sem=send_sem.at[r],
            recv_sem=recv_sem.at[r],
            device_id={"seq": (group + GROUPS - r) % GROUPS * across + column},
            device_id_type=pl.DeviceIdType.MESH,
        )

    def send_mass(p):
        return pltpu.make_async_remote_copy(
            src_ref=masses.at[0],
            dst_ref=masses.at[p],
            send_sem=mass_send.at[p],
            recv_sem=mass_recv.at[p],
            device_id={"seq": (me + p) % seq_count},
            device_id_type=pl.DeviceIdType.MESH,
        )

    def work(t, carry):
        r = (t // tiles + 1) % GROUPS
        first = pl.multiple_of(t % tiles * tile, tile)
        q = q_ref[r, pl.ds(first, tile), :]
        weigh = q[:, 0:1].astype(F32)
        result = jnp.zeros((tile, wide), F32)
        for h in range(heads):
            mine = (lane >= (h + 1) * HEAD) & (lane < (h + 2) * HEAD)
            qh = jnp.where(mine, q, jnp.zeros_like(q))
            parts = []
            o = jnp.zeros((tile, wide), F32)
            for c in range(0, keys, chunk):
                s = lax.dot_general(qh, k_ref[c : c + chunk, :], NT, preferred_element_type=F32)
                e = jnp.exp2(s * EXP2_SCALE)
                o += jnp.dot(e.astype(BF16), v_ref[c : c + chunk, :], preferred_element_type=F32)
                parts.append(e)
            inverse = 1.0 / o[:, part : part + 1]
            result = jnp.where((lane >= h * HEAD) & (lane < (h + 1) * HEAD), o * inverse, result)
            weight = inverse * weigh
            for c, e in zip(range(0, keys, chunk), parts):
                mass[:, c : c + chunk] += jnp.sum((e * weight).reshape(tile // 8, 8, chunk), axis=0)
        context[r, pl.ds(first, tile), :] = result[:, :part].astype(BF16)

        @pl.when(t == tiles - 1)
        def _():
            pl.semaphore_wait(barrier, seq_count - 1)

        @pl.when((t % tiles == tiles - 1) & (t < (GROUPS - 1) * tiles))
        def _():
            send_back(r).start()

        return carry

    lax.fori_loop(0, GROUPS * tiles, work, 0)
    masses[0, :, :keys] = jnp.sum(mass[...], axis=0, keepdims=True)
    masses[0, :, keys:] = count_ref[...]
    for p in range(1, seq_count):
        send_mass(p).start()

    def weights(r):
        return w_ref[pl.ds(pl.multiple_of((group + r) % GROUPS * part, part), part), :]

    total = middle_ref[...].astype(F32)
    total += jnp.dot(context[0], weights(0), preferred_element_type=F32)
    for r in range(1, GROUPS):
        send_back(r).wait()
        total += jnp.dot(landed[r], weights(r), preferred_element_type=F32)
    o_ref[...] = total.astype(BF16)
    for p in range(1, seq_count):
        send_mass(p).wait()
    mass_ref[...] = jnp.sum(masses[...], axis=0)


def cross_attend(seq_count, count, queries, key_rows, value_rows, middle, x_out):
    groups, rows, wide = queries.shape
    keys = key_rows.shape[0]
    part = wide - HEAD
    vmem = pl.BlockSpec(memory_space=pltpu.VMEM)
    return pl.pallas_call(
        functools.partial(cross_kernel, seq_count, 512),
        out_shape=(
            jax.ShapeDtypeStruct(middle.shape, BF16),
            jax.ShapeDtypeStruct((1, keys + 128), F32),
        ),
        in_specs=[vmem] * 6,
        out_specs=(vmem, vmem),
        scratch_shapes=[
            pltpu.VMEM((groups, rows, part), BF16),
            pltpu.VMEM((groups, rows, part), BF16),
            pltpu.VMEM((8, keys), F32),
            pltpu.VMEM((seq_count, 1, keys + 128), F32),
            pltpu.SemaphoreType.DMA((groups,)),
            pltpu.SemaphoreType.DMA((groups,)),
            pltpu.SemaphoreType.DMA((seq_count,)),
            pltpu.SemaphoreType.DMA((seq_count,)),
        ],
        compiler_params=pltpu.CompilerParams(
            vmem_limit_bytes=48 * 1024 * 1024, collective_id=0, has_side_effects=True
        ),
        cost_estimate=pl.CostEstimate(
            flops=16 * groups * rows * keys * part,
            bytes_accessed=4 * keys * wide + 4 * rows * wide,
            transcendentals=3 * groups * rows * keys,
        ),
    )(count, queries, key_rows, value_rows, middle, x_out)


def local(
    hidden, token_ids, w_query, w_keyval, w_out, x_query, x_out, shortlist, code_row, code_cache
):
    doc_hidden = hidden[0]
    doc_tokens = token_ids[0]
    tok_rows, width = doc_hidden.shape
    seq_count = lax.axis_size("seq")
    doc_count = lax.axis_size("doc")
    devices = seq_count * doc_count
    across = seq_count // GROUPS
    seq_index = lax.axis_index("seq")
    doc_index = lax.axis_index("doc")
    me = doc_index * seq_count + seq_index
    group = seq_index // across
    cand_count = shortlist.shape[1]
    code_dev = code_cache.shape[0]
    capacity = 8 * cand_count // (5 * devices)
    slots = devices * capacity
    part = width // GROUPS

    cache_rows = code_row[shortlist[0]]
    relative = [cache_rows]
    for r in range(1, doc_count):
        relative.append(
            lax.ppermute(cache_rows, "doc", [(i, (i + r) % doc_count) for i in range(doc_count)])
        )
    relative = jnp.stack(relative)
    docs = jnp.arange(doc_count, dtype=jnp.int32)
    source = (doc_index - docs) % doc_count
    rows_of = jnp.sum(
        jnp.where((source[None, :] == docs[:, None])[:, :, None], relative[None], 0), axis=1
    )
    order = jnp.arange(cand_count, dtype=jnp.int32)
    before = (order[:, None] < order[None, :]).astype(BF16)
    held = rows_of // code_dev == me
    rank = jnp.dot(held.astype(BF16), before, preferred_element_type=F32).astype(jnp.int32)
    slot = jnp.arange(capacity, dtype=jnp.int32)
    request = jnp.sum(
        jnp.where(
            held[:, None, :] & (rank[:, None, :] == slot[None, :, None]),
            (rows_of % code_dev)[:, None, :],
            0,
        ),
        axis=2,
    )
    picked = gather_rows(request.reshape(-1), code_cache, capacity)
    picked = picked.reshape(devices, DESC // across * capacity, 2 * part)
    arrived = lax.all_to_all(picked, ("doc", "seq"), split_axis=0, concat_axis=0, tiled=True)

    owner = cache_rows // code_dev
    onehot = (owner[:, None] == jnp.arange(devices, dtype=jnp.int32)[None, :]).astype(BF16)
    ahead = jnp.dot(before.T, onehot, preferred_element_type=F32)
    slot_rank = jnp.sum(ahead * onehot, axis=1).astype(jnp.int32)
    slot_index = owner * capacity + slot_rank
    spot = jnp.arange(slots * DESC // across, dtype=jnp.int32)
    inner = DESC // across * capacity
    spot_slot = spot // inner * capacity + spot % capacity
    spot_desc = spot // capacity % (DESC // across)
    descs = jnp.arange(DESC // across, dtype=jnp.int32)
    choose = (slot_index[None, :, None] == spot_slot[None, None, :]) & (
        descs[:, None, None] == spot_desc[None, None, :]
    )
    choose = choose.astype(BF16).reshape(DESC // across * cand_count, -1)

    normed = layer_norm(doc_hidden.astype(F32)).astype(BF16)
    query = jnp.dot(normed, w_query, preferred_element_type=F32).astype(BF16)
    keyval = jnp.dot(normed, w_keyval, preferred_element_type=F32).astype(BF16)
    up = [(i, i + 1) for i in range(seq_count - 1)]
    down = [(i + 1, i) for i in range(seq_count - 1)]
    live = (doc_tokens != 0).astype(F32)
    low_live = lax.ppermute(live[tok_rows - HALF_WIN :], "seq", up)
    high_live = lax.ppermute(live[:HALF_WIN], "seq", down)
    low = lax.ppermute(keyval[tok_rows - HALF_WIN :], "seq", up)
    high = lax.ppermute(keyval[:HALF_WIN], "seq", down)
    valid = jnp.concatenate([low_live, live, high_live])[None]
    context = window_attend(valid, query, low, keyval, high)
    middle = (
        doc_hidden.astype(F32) + jnp.dot(context, w_out, preferred_element_type=F32)
    ).astype(BF16)
    middle_wide = middle.astype(F32)
    cross_normed = layer_norm(middle_wide).astype(BF16)
    wide = part + HEAD
    spread = jnp.pad(x_query.reshape(width, GROUPS, part), ((0, 0), (0, 0), (HEAD, 0)))
    spread = spread.reshape(width, GROUPS * wide)
    flag = (jnp.arange(GROUPS * wide) % wide < HEAD)[None, :]
    cross_query = jnp.dot(cross_normed, spread, preferred_element_type=F32)
    cross_query = jnp.where(flag, live[:, None], cross_query).astype(BF16)

    def turn(r):
        return [
            (i, (i // across + r) % GROUPS * across + i % across) for i in range(seq_count)
        ]

    def piece(array, g):
        return lax.dynamic_slice_in_dim(array, g * wide, wide, axis=1)

    queries = [piece(cross_query, group)]
    for r in range(1, GROUPS):
        queries.append(
            lax.ppermute(piece(cross_query, (group + r) % GROUPS), "seq", turn(r))
        )

    arrived = arrived.reshape(-1, 2 * part)
    own_rows = jnp.dot(choose, arrived, preferred_element_type=F32).astype(BF16)
    all_rows = [own_rows]
    for r in range(1, across):
        step = [(i, i // across * across + (i % across + r) % across) for i in range(seq_count)]
        all_rows.append(lax.ppermute(own_rows, "seq", step))
    all_rows = jnp.concatenate(all_rows)
    column = jnp.arange(part + HEAD)
    value_rows = jnp.where(
        column[None, :] < part, all_rows[:, : part + HEAD], jnp.ones((), BF16)
    )
    key_rows = all_rows[:, part - HEAD :]

    count = jnp.full((1, 128), jnp.sum(live))
    refined, mass = cross_attend(
        seq_count, count, jnp.stack(queries), key_rows, value_rows, middle, x_out
    )
    cand_mass = jnp.sum(mass[0, :-128].reshape(DESC, cand_count), axis=0)
    cand_score = cand_count * cand_mass / (HEADS * mass[0, -1])
    return (refined[None], cand_score[None])


def solution(mesh):
    return jax.shard_map(
        local,
        mesh=mesh,
        in_specs=(
            P("doc", "seq", None),
            P("doc", "seq"),
            P(),
            P(),
            P(),
            P(),
            P(),
            P("doc", None),
            P(),
            P(("doc", "seq"), None, None, None),
        ),
        out_specs=(P("doc", "seq", None), P("doc", None)),
        check_vma=False,
    )
```

```python
import functools
import math

import jax
import jax.numpy as jnp
from jax import lax
from jax.experimental import pallas as pl
from jax.experimental.pallas import tpu as pltpu
from jax.sharding import PartitionSpec as P

HEADS = 12
HEAD = 64
HALF_WIN = 256
DESC = 8
GROUPS = 4
CHUNKS = 2
EXP2_SCALE = math.log2(math.e) / math.sqrt(HEAD)
F32 = jnp.float32
BF16 = jnp.bfloat16
NT = (((1,), (1,)), ((), ()))


def layer_norm(values):
    centered = values - jnp.mean(values, axis=-1, keepdims=True)
    spread = jnp.mean(centered * centered, axis=-1, keepdims=True)
    return centered * lax.rsqrt(spread + 1e-05)


def window_kernel(valid_ref, q_ref, kl_ref, ko_ref, kh_ref, vl_ref, vo_ref, vh_ref, o_ref, bias):
    rows = q_ref.shape[0]
    half = HALF_WIN
    blocks = rows // half
    width = 3 * half

    @pl.when(pl.program_id(0) == 0)
    def _():
        for b in range(blocks):
            i = lax.broadcasted_iota(jnp.int32, (half, width), 0)
            j = lax.broadcasted_iota(jnp.int32, (half, width), 1)
            ok = valid_ref[:, b * half : b * half + width] > 0.0
            allowed = (j >= i) & (j <= i + 2 * half) & (ok | (j == i + half))
            bias[b] = jnp.where(allowed, 0.0, -1e30)

    k = jnp.concatenate([kl_ref[...], ko_ref[...], kh_ref[...]], axis=0)
    v = jnp.concatenate([vl_ref[...], vo_ref[...], vh_ref[...]], axis=0)
    v = jnp.concatenate([v, jnp.ones_like(v)], axis=1)
    lane = lax.broadcasted_iota(jnp.int32, (half, 2 * HEAD), 1)
    for b in range(blocks):
        q = q_ref[b * half : (b + 1) * half, :]
        kb = k[b * half : b * half + width]
        vb = v[b * half : b * half + width]
        outs = []
        for h in range(2):
            mine = (lane >= h * HEAD) & (lane < (h + 1) * HEAD)
            s = lax.dot_general(
                jnp.where(mine, q, jnp.zeros_like(q)), kb, NT, preferred_element_type=F32
            )
            e = jnp.exp2(s * EXP2_SCALE + bias[b])
            o = jnp.dot(e.astype(BF16), vb, preferred_element_type=F32)
            outs.append(o[:, : 2 * HEAD] / o[:, 2 * HEAD :])
        o_ref[b * half : (b + 1) * half, :] = jnp.where(lane < HEAD, outs[0], outs[1]).astype(BF16)


def window_attend(valid, query, low, own, high):
    rows, width = query.shape
    pairs = width // (2 * HEAD)
    span = rows + 2 * HALF_WIN

    def cols(r, first):
        return pl.BlockSpec((r, 2 * HEAD), lambda p: (0, p + first))

    return pl.pallas_call(
        window_kernel,
        grid=(pairs,),
        out_shape=jax.ShapeDtypeStruct((rows, width), BF16),
        in_specs=[
            pl.BlockSpec((1, span), lambda p: (0, 0)),
            cols(rows, 0),
            cols(HALF_WIN, 0),
            cols(rows, 0),
            cols(HALF_WIN, 0),
            cols(HALF_WIN, pairs),
            cols(rows, pairs),
            cols(HALF_WIN, pairs),
        ],
        out_specs=cols(rows, 0),
        scratch_shapes=[pltpu.VMEM((rows // HALF_WIN, HALF_WIN, 3 * HALF_WIN), F32)],
        compiler_params=pltpu.CompilerParams(vmem_limit_bytes=48 * 1024 * 1024),
        cost_estimate=pl.CostEstimate(
            flops=8 * rows * 3 * HALF_WIN * width,
            bytes_accessed=8 * rows * width,
            transcendentals=rows * 3 * HALF_WIN * HEADS,
        ),
    )(valid, query, low, own, high, low, own, high)


def gather_kernel(docs, capacity, request_ref, cache_ref, order_ref, *refs):
    *outs, held, sems = refs
    count = docs * capacity
    step = 2 * DESC
    part = outs[0].shape[-1] // 2

    def fetch(i):
        row = pl.multiple_of(request_ref[i] * step, step)
        return pltpu.make_async_copy(
            cache_ref.at[pl.ds(row, step)], held.at[pl.ds(i * step, step)], sems.at[i]
        )

    for i in range(count):
        fetch(i).start()
    rows = capacity * step
    half = capacity * DESC
    for d in range(docs):
        for i in range(d * capacity, (d + 1) * capacity):
            fetch(i).wait()
        ordered = jnp.dot(
            order_ref[...], held[d * rows : (d + 1) * rows, :], preferred_element_type=F32
        ).astype(BF16)
        for g in range(GROUPS):
            cols = slice(g * part, (g + 1) * part)
            both = jnp.concatenate([ordered[:half, cols], ordered[half:, cols]], axis=1)
            size = half // len(outs)
            for c, out_ref in enumerate(outs):
                out_ref[d, g] = both[c * size : (c + 1) * size]


def gather_rows(request, cache, capacity, across):
    docs = request.shape[0] // capacity
    codes, pair, desc, width = cache.shape
    part = width // GROUPS
    rows = capacity * pair * desc
    out = jnp.arange(rows)
    inner = desc // across // CHUNKS
    chunk = out // (desc * capacity // CHUNKS) % CHUNKS
    column = out // (inner * capacity) % across
    position = (column * CHUNKS + chunk) * inner + out // capacity % inner
    source = out % capacity * (2 * desc) + (1 - out // (desc * capacity)) * desc + position
    order = (source[:, None] == out[None, :]).astype(BF16)
    return pl.pallas_call(
        functools.partial(gather_kernel, docs, capacity),
        out_shape=[jax.ShapeDtypeStruct((docs, GROUPS, rows // 2 // CHUNKS, 2 * part), BF16)]
        * CHUNKS,
        in_specs=[
            pl.BlockSpec(memory_space=pltpu.SMEM),
            pl.BlockSpec(memory_space=pl.ANY),
            pl.BlockSpec(memory_space=pltpu.VMEM),
        ],
        out_specs=[pl.BlockSpec(memory_space=pltpu.VMEM)] * CHUNKS,
        scratch_shapes=[
            pltpu.VMEM((docs * rows, width), BF16),
            pltpu.SemaphoreType.DMA((docs * capacity,)),
        ],
        compiler_params=pltpu.CompilerParams(vmem_limit_bytes=48 * 1024 * 1024),
        cost_estimate=pl.CostEstimate(
            flops=2 * docs * rows * rows * width,
            bytes_accessed=4 * docs * rows * width,
            transcendentals=0,
        ),
    )(request, cache.reshape(codes * pair * desc, width), order)


def cross_kernel(
    seq_count,
    chunk,
    pieces,
    count_ref,
    middle_ref,
    w_ref,
    *refs,
):
    queries, refs = refs[:GROUPS], refs[GROUPS:]
    rows_in, refs = refs[:pieces], refs[pieces:]
    o_ref, mass_ref, q_ref, k_ref, v_ref, context, landed, mass, masses = refs[:9]
    send_sem, recv_sem, mass_send, mass_recv = refs[9:]
    me = lax.axis_index("seq")
    across = seq_count // GROUPS
    group = me // across
    column = me % across
    keys, wide = k_ref.shape
    tile = 256
    tiles = q_ref.shape[1] // tile
    part = wide - HEAD
    heads = part // HEAD
    lane = lax.broadcasted_iota(jnp.int32, (tile, wide), 1)

    barrier = pltpu.get_barrier_semaphore()
    for p in range(1, seq_count):
        pl.semaphore_signal(
            barrier,
            inc=1,
            device_id={"seq": (me + p) % seq_count},
            device_id_type=pl.DeviceIdType.MESH,
        )
    mass[...] = jnp.zeros_like(mass)
    size = keys // pieces
    for n, piece in enumerate(rows_in):
        k_ref[n * size : (n + 1) * size, :] = piece[:, part - HEAD :]
        ahead = lax.broadcasted_iota(jnp.int32, (size, wide), 1) < part
        v_ref[n * size : (n + 1) * size, :] = jnp.where(ahead, piece[:, :wide], jnp.ones((), BF16))
    for r, query in enumerate(queries):
        q_ref[r] = query[...]

    def send_back(r):
        return pltpu.make_async_remote_copy(
            src_ref=context.at[r],
            dst_ref=landed.at[r],
            send_sem=send_sem.at[r],
            recv_sem=recv_sem.at[r],
            device_id={"seq": (group + GROUPS - r) % GROUPS * across + column},
            device_id_type=pl.DeviceIdType.MESH,
        )

    def send_mass(p):
        return pltpu.make_async_remote_copy(
            src_ref=masses.at[0],
            dst_ref=masses.at[p],
            send_sem=mass_send.at[p],
            recv_sem=mass_recv.at[p],
            device_id={"seq": (me + p) % seq_count},
            device_id_type=pl.DeviceIdType.MESH,
        )

    def work(t, carry):
        r = (t // tiles + 1) % GROUPS
        first = pl.multiple_of(t % tiles * tile, tile)
        q = q_ref[r, pl.ds(first, tile), :]
        weigh = q[:, 0:1].astype(F32)
        result = jnp.zeros((tile, wide), F32)
        for h in range(heads):
            mine = (lane >= (h + 1) * HEAD) & (lane < (h + 2) * HEAD)
            qh = jnp.where(mine, q, jnp.zeros_like(q))
            parts = []
            o = jnp.zeros((tile, wide), F32)
            for c in range(0, keys, chunk):
                s = lax.dot_general(qh, k_ref[c : c + chunk, :], NT, preferred_element_type=F32)
                e = jnp.exp2(s * EXP2_SCALE)
                o += jnp.dot(e.astype(BF16), v_ref[c : c + chunk, :], preferred_element_type=F32)
                parts.append(e)
            inverse = 1.0 / o[:, part : part + 1]
            result = jnp.where((lane >= h * HEAD) & (lane < (h + 1) * HEAD), o * inverse, result)
            weight = inverse * weigh
            for c, e in zip(range(0, keys, chunk), parts):
                mass[:, c : c + chunk] += jnp.sum((e * weight).reshape(tile // 8, 8, chunk), axis=0)
        context[r, pl.ds(first, tile), :] = result[:, :part].astype(BF16)

        @pl.when(t == tiles - 1)
        def _():
            pl.semaphore_wait(barrier, seq_count - 1)

        @pl.when((t % tiles == tiles - 1) & (t < (GROUPS - 1) * tiles))
        def _():
            send_back(r).start()

        return carry

    lax.fori_loop(0, GROUPS * tiles, work, 0)
    masses[0, :, :keys] = jnp.sum(mass[...], axis=0, keepdims=True)
    masses[0, :, keys:] = count_ref[...]
    for p in range(1, seq_count):
        send_mass(p).start()

    def weights(r):
        return w_ref[pl.ds(pl.multiple_of((group + r) % GROUPS * part, part), part), :]

    total = middle_ref[...].astype(F32)
    total += jnp.dot(context[0], weights(0), preferred_element_type=F32)
    for r in range(1, GROUPS):
        send_back(r).wait()
        total += jnp.dot(landed[r], weights(r), preferred_element_type=F32)
    o_ref[...] = total.astype(BF16)
    for p in range(1, seq_count):
        send_mass(p).wait()
    mass_ref[...] = jnp.sum(masses[...], axis=0)


def cross_attend(seq_count, count, queries, pieces, middle, x_out):
    groups = len(queries)
    rows, wide = queries[0].shape
    keys = sum(piece.shape[0] for piece in pieces)
    part = wide - HEAD
    vmem = pl.BlockSpec(memory_space=pltpu.VMEM)
    return pl.pallas_call(
        functools.partial(cross_kernel, seq_count, 512, len(pieces)),
        out_shape=(
            jax.ShapeDtypeStruct(middle.shape, BF16),
            jax.ShapeDtypeStruct((1, keys + 128), F32),
        ),
        in_specs=[vmem] * (3 + groups + len(pieces)),
        out_specs=(vmem, vmem),
        scratch_shapes=[
            pltpu.VMEM((groups, rows, wide), BF16),
            pltpu.VMEM((keys, wide), BF16),
            pltpu.VMEM((keys, wide), BF16),
            pltpu.VMEM((groups, rows, part), BF16),
            pltpu.VMEM((groups, rows, part), BF16),
            pltpu.VMEM((8, keys), F32),
            pltpu.VMEM((seq_count, 1, keys + 128), F32),
            pltpu.SemaphoreType.DMA((groups,)),
            pltpu.SemaphoreType.DMA((groups,)),
            pltpu.SemaphoreType.DMA((seq_count,)),
            pltpu.SemaphoreType.DMA((seq_count,)),
        ],
        compiler_params=pltpu.CompilerParams(
            vmem_limit_bytes=48 * 1024 * 1024, collective_id=0, has_side_effects=True
        ),
        cost_estimate=pl.CostEstimate(
            flops=16 * groups * rows * keys * part,
            bytes_accessed=4 * keys * wide + 4 * rows * wide,
            transcendentals=3 * groups * rows * keys,
        ),
    )(count, middle, x_out, *queries, *pieces)


def local(
    hidden, token_ids, w_query, w_keyval, w_out, x_query, x_out, shortlist, code_row, code_cache
):
    doc_hidden = hidden[0]
    doc_tokens = token_ids[0]
    tok_rows, width = doc_hidden.shape
    seq_count = lax.axis_size("seq")
    doc_count = lax.axis_size("doc")
    devices = seq_count * doc_count
    across = seq_count // GROUPS
    seq_index = lax.axis_index("seq")
    doc_index = lax.axis_index("doc")
    me = doc_index * seq_count + seq_index
    group = seq_index // across
    cand_count = shortlist.shape[1]
    code_dev = code_cache.shape[0]
    capacity = 8 * cand_count // (5 * devices)
    slots = devices * capacity
    part = width // GROUPS

    cache_rows = code_row[shortlist[0]]
    relative = [cache_rows]
    for r in range(1, doc_count):
        relative.append(
            lax.ppermute(cache_rows, "doc", [(i, (i + r) % doc_count) for i in range(doc_count)])
        )
    relative = jnp.stack(relative)
    docs = jnp.arange(doc_count, dtype=jnp.int32)
    source = (doc_index - docs) % doc_count
    rows_of = jnp.sum(
        jnp.where((source[None, :] == docs[:, None])[:, :, None], relative[None], 0), axis=1
    )
    order = jnp.arange(cand_count, dtype=jnp.int32)
    before = (order[:, None] < order[None, :]).astype(BF16)
    held = rows_of // code_dev == me
    rank = jnp.dot(held.astype(BF16), before, preferred_element_type=F32).astype(jnp.int32)
    slot = jnp.arange(capacity, dtype=jnp.int32)
    request = jnp.sum(
        jnp.where(
            held[:, None, :] & (rank[:, None, :] == slot[None, :, None]),
            (rows_of % code_dev)[:, None, :],
            0,
        ),
        axis=2,
    )
    picked = gather_rows(request.reshape(-1), code_cache, capacity, across)
    inner = DESC // across // CHUNKS
    arrived = []
    for chunk in picked:
        chunk = chunk.reshape(devices, inner * capacity, 2 * part)
        if arrived:
            chunk, arrived[-1] = lax.optimization_barrier((chunk, arrived[-1]))
        arrived.append(
            lax.all_to_all(chunk, ("doc", "seq"), split_axis=0, concat_axis=0, tiled=True)
        )

    owner = cache_rows // code_dev
    onehot = (owner[:, None] == jnp.arange(devices, dtype=jnp.int32)[None, :]).astype(BF16)
    ahead = jnp.dot(before.T, onehot, preferred_element_type=F32)
    slot_rank = jnp.sum(ahead * onehot, axis=1).astype(jnp.int32)
    slot_index = owner * capacity + slot_rank
    spot = jnp.arange(slots * inner, dtype=jnp.int32)
    spot_slot = spot // (inner * capacity) * capacity + spot % capacity
    descs = jnp.arange(inner, dtype=jnp.int32)
    choose = (slot_index[None, :, None] == spot_slot[None, None, :]) & (
        descs[:, None, None] == (spot // capacity % inner)[None, None, :]
    )
    choose = choose.astype(BF16).reshape(inner * cand_count, -1)

    normed = layer_norm(doc_hidden.astype(F32)).astype(BF16)
    query = jnp.dot(normed, w_query, preferred_element_type=F32).astype(BF16)
    keyval = jnp.dot(normed, w_keyval, preferred_element_type=F32).astype(BF16)
    up = [(i, i + 1) for i in range(seq_count - 1)]
    down = [(i + 1, i) for i in range(seq_count - 1)]
    live = (doc_tokens != 0).astype(F32)
    flagged = jnp.concatenate(
        [keyval, jnp.broadcast_to(live.astype(BF16)[:, None], (tok_rows, 2 * HEAD))], axis=1
    )
    low = lax.ppermute(flagged[tok_rows - HALF_WIN :], "seq", up)
    high = lax.ppermute(flagged[:HALF_WIN], "seq", down)
    valid = jnp.concatenate([low[:, 2 * width], live.astype(BF16), high[:, 2 * width]])
    valid = valid.astype(F32)[None]
    context = window_attend(valid, query, low, keyval, high)
    middle = (
        doc_hidden.astype(F32) + jnp.dot(context, w_out, preferred_element_type=F32)
    ).astype(BF16)
    middle_wide = middle.astype(F32)
    cross_normed = layer_norm(middle_wide).astype(BF16)
    wide = part + HEAD
    blank = jnp.zeros((width, HEAD), BF16)
    spread = []
    for g in range(GROUPS):
        spread += [blank, x_query[:, g * part : (g + 1) * part]]
    spread = jnp.concatenate(spread, axis=1)
    flag = (jnp.arange(GROUPS * wide) % wide < HEAD)[None, :]
    cross_query = jnp.dot(cross_normed, spread, preferred_element_type=F32)
    cross_query = jnp.where(flag, live[:, None], cross_query).astype(BF16)

    def turn(r):
        return [
            (i, (i // across + r) % GROUPS * across + i % across) for i in range(seq_count)
        ]

    def piece(array, g):
        return lax.dynamic_slice_in_dim(array, g * wide, wide, axis=1)

    queries = [piece(cross_query, group)]
    for r in range(1, GROUPS):
        queries.append(
            lax.ppermute(piece(cross_query, (group + r) % GROUPS), "seq", turn(r))
        )

    pieces = []
    for chunk in arrived:
        own_rows = jnp.dot(
            choose, chunk.reshape(-1, 2 * part), preferred_element_type=F32
        ).astype(BF16)
        pieces.append(own_rows)
        for r in range(1, across):
            step = [(i, i // across * across + (i % across + r) % across) for i in range(seq_count)]
            pieces.append(lax.ppermute(own_rows, "seq", step))

    count = jnp.full((1, 128), jnp.sum(live))
    refined, mass = cross_attend(
        seq_count, count, queries, pieces, middle, x_out
    )
    cand_mass = jnp.sum(mass[0, :-128].reshape(DESC, cand_count), axis=0)
    cand_score = cand_count * cand_mass / (HEADS * mass[0, -1])
    return (refined[None], cand_score[None])


def solution(mesh):
    return jax.shard_map(
        local,
        mesh=mesh,
        in_specs=(
            P("doc", "seq", None),
            P("doc", "seq"),
            P(),
            P(),
            P(),
            P(),
            P(),
            P("doc", None),
            P(),
            P(("doc", "seq"), None, None, None),
        ),
        out_specs=(P("doc", "seq", None), P("doc", None)),
        check_vma=False,
    )
```

```python
import functools
import math

import jax
import jax.numpy as jnp
from jax import lax
from jax.experimental import pallas as pl
from jax.experimental.pallas import tpu as pltpu
from jax.sharding import PartitionSpec as P

HEADS = 12
HEAD = 64
HALF_WIN = 256
DESC = 8
GROUPS = 4
CHUNKS = 1
EXP2_SCALE = math.log2(math.e) / math.sqrt(HEAD)
F32 = jnp.float32
BF16 = jnp.bfloat16
NT = (((1,), (1,)), ((), ()))


def layer_norm(values):
    centered = values - jnp.mean(values, axis=-1, keepdims=True)
    spread = jnp.mean(centered * centered, axis=-1, keepdims=True)
    return centered * lax.rsqrt(spread + 1e-05)


def window_kernel(valid_ref, q_ref, k_ref, v_ref, o_ref, bias):
    rows = q_ref.shape[0]
    half = HALF_WIN
    blocks = rows // half
    width = 3 * half

    @pl.when(pl.program_id(0) == 0)
    def _():
        for b in range(blocks):
            i = lax.broadcasted_iota(jnp.int32, (half, width), 0)
            j = lax.broadcasted_iota(jnp.int32, (half, width), 1)
            ok = valid_ref[:, b * half : b * half + width] > 0.0
            allowed = (j >= i) & (j <= i + 2 * half) & (ok | (j == i + half))
            bias[b] = jnp.where(allowed, 0.0, -1e30)

    k = k_ref[...]
    v = v_ref[...]
    v = jnp.concatenate([v, jnp.ones_like(v)], axis=1)
    lane = lax.broadcasted_iota(jnp.int32, (half, 2 * HEAD), 1)
    for b in range(blocks):
        q = q_ref[b * half : (b + 1) * half, :]
        kb = k[b * half : b * half + width]
        vb = v[b * half : b * half + width]
        outs = []
        for h in range(2):
            mine = (lane >= h * HEAD) & (lane < (h + 1) * HEAD)
            s = lax.dot_general(
                jnp.where(mine, q, jnp.zeros_like(q)), kb, NT, preferred_element_type=F32
            )
            e = jnp.exp2(s * EXP2_SCALE + bias[b])
            o = jnp.dot(e.astype(BF16), vb, preferred_element_type=F32)
            outs.append(o[:, : 2 * HEAD] / o[:, 2 * HEAD :])
        o_ref[b * half : (b + 1) * half, :] = jnp.where(lane < HEAD, outs[0], outs[1]).astype(BF16)


def window_attend(valid, query, keyval):
    rows, width = query.shape
    pairs = width // (2 * HEAD)
    span = rows + 2 * HALF_WIN

    def cols(r, first):
        return pl.BlockSpec((r, 2 * HEAD), lambda p: (0, p + first))

    return pl.pallas_call(
        window_kernel,
        grid=(pairs,),
        out_shape=jax.ShapeDtypeStruct((rows, width), BF16),
        in_specs=[
            pl.BlockSpec((1, span), lambda p: (0, 0)),
            cols(rows, 0),
            cols(span, 0),
            cols(span, pairs),
        ],
        out_specs=cols(rows, 0),
        scratch_shapes=[pltpu.VMEM((rows // HALF_WIN, HALF_WIN, 3 * HALF_WIN), F32)],
        compiler_params=pltpu.CompilerParams(vmem_limit_bytes=48 * 1024 * 1024),
        cost_estimate=pl.CostEstimate(
            flops=8 * rows * 3 * HALF_WIN * width,
            bytes_accessed=8 * rows * width,
            transcendentals=rows * 3 * HALF_WIN * HEADS,
        ),
    )(valid, query, keyval, keyval)


def gather_kernel(docs, capacity, request_ref, cache_ref, order_ref, *refs):
    *outs, held, sems = refs
    count = docs * capacity
    step = 2 * DESC
    part = outs[0].shape[-1] // 2

    def fetch(i):
        row = pl.multiple_of(request_ref[i] * step, step)
        return pltpu.make_async_copy(
            cache_ref.at[pl.ds(row, step)], held.at[pl.ds(i * step, step)], sems.at[i]
        )

    for i in range(count):
        fetch(i).start()
    rows = capacity * step
    half = capacity * DESC
    for d in range(docs):
        for i in range(d * capacity, (d + 1) * capacity):
            fetch(i).wait()
        ordered = jnp.dot(
            order_ref[...], held[d * rows : (d + 1) * rows, :], preferred_element_type=F32
        ).astype(BF16)
        for g in range(GROUPS):
            cols = slice(g * part, (g + 1) * part)
            both = jnp.concatenate([ordered[:half, cols], ordered[half:, cols]], axis=1)
            size = half // len(outs)
            for c, out_ref in enumerate(outs):
                out_ref[d, g] = both[c * size : (c + 1) * size]


def gather_rows(request, cache, capacity, across):
    docs = request.shape[0] // capacity
    codes, pair, desc, width = cache.shape
    part = width // GROUPS
    rows = capacity * pair * desc
    out = jnp.arange(rows)
    inner = desc // across // CHUNKS
    chunk = out // (desc * capacity // CHUNKS) % CHUNKS
    column = out // (inner * capacity) % across
    position = (column * CHUNKS + chunk) * inner + out // capacity % inner
    source = out % capacity * (2 * desc) + (1 - out // (desc * capacity)) * desc + position
    order = (source[:, None] == out[None, :]).astype(BF16)
    return pl.pallas_call(
        functools.partial(gather_kernel, docs, capacity),
        out_shape=[jax.ShapeDtypeStruct((docs, GROUPS, rows // 2 // CHUNKS, 2 * part), BF16)]
        * CHUNKS,
        in_specs=[
            pl.BlockSpec(memory_space=pltpu.SMEM),
            pl.BlockSpec(memory_space=pl.ANY),
            pl.BlockSpec(memory_space=pltpu.VMEM),
        ],
        out_specs=[pl.BlockSpec(memory_space=pltpu.VMEM)] * CHUNKS,
        scratch_shapes=[
            pltpu.VMEM((docs * rows, width), BF16),
            pltpu.SemaphoreType.DMA((docs * capacity,)),
        ],
        compiler_params=pltpu.CompilerParams(vmem_limit_bytes=48 * 1024 * 1024),
        cost_estimate=pl.CostEstimate(
            flops=2 * docs * rows * rows * width,
            bytes_accessed=4 * docs * rows * width,
            transcendentals=0,
        ),
    )(request, cache.reshape(codes * pair * desc, width), order)


def cross_kernel(
    seq_count,
    chunk,
    pieces,
    count_ref,
    middle_ref,
    w_ref,
    *refs,
):
    queries, refs = refs[:GROUPS], refs[GROUPS:]
    rows_in, refs = refs[:pieces], refs[pieces:]
    o_ref, mass_ref, q_ref, k_ref, v_ref, context, landed, mass, masses = refs[:9]
    send_sem, recv_sem, mass_send, mass_recv = refs[9:]
    me = lax.axis_index("seq")
    across = seq_count // GROUPS
    group = me // across
    column = me % across
    keys, wide = k_ref.shape
    tile = 256
    tiles = q_ref.shape[1] // tile
    part = wide - HEAD
    heads = part // HEAD
    lane = lax.broadcasted_iota(jnp.int32, (tile, wide), 1)

    barrier = pltpu.get_barrier_semaphore()
    for p in range(1, seq_count):
        pl.semaphore_signal(
            barrier,
            inc=1,
            device_id={"seq": (me + p) % seq_count},
            device_id_type=pl.DeviceIdType.MESH,
        )
    mass[...] = jnp.zeros_like(mass)
    size = keys // pieces
    for n, piece in enumerate(rows_in):
        k_ref[n * size : (n + 1) * size, :] = piece[:, part - HEAD :]
        ahead = lax.broadcasted_iota(jnp.int32, (size, wide), 1) < part
        v_ref[n * size : (n + 1) * size, :] = jnp.where(ahead, piece[:, :wide], jnp.ones((), BF16))
    for r, query in enumerate(queries):
        q_ref[r] = query[...]

    def send_back(r):
        return pltpu.make_async_remote_copy(
            src_ref=context.at[r],
            dst_ref=landed.at[r],
            send_sem=send_sem.at[r],
            recv_sem=recv_sem.at[r],
            device_id={"seq": (group + GROUPS - r) % GROUPS * across + column},
            device_id_type=pl.DeviceIdType.MESH,
        )

    def send_mass(p):
        return pltpu.make_async_remote_copy(
            src_ref=masses.at[0],
            dst_ref=masses.at[p],
            send_sem=mass_send.at[p],
            recv_sem=mass_recv.at[p],
            device_id={"seq": (me + p) % seq_count},
            device_id_type=pl.DeviceIdType.MESH,
        )

    def work(t, carry):
        r = (t // tiles + 1) % GROUPS
        first = pl.multiple_of(t % tiles * tile, tile)
        q = q_ref[r, pl.ds(first, tile), :]
        weigh = q[:, 0:1].astype(F32)
        result = jnp.zeros((tile, wide), F32)
        for h in range(heads):
            mine = (lane >= (h + 1) * HEAD) & (lane < (h + 2) * HEAD)
            qh = jnp.where(mine, q, jnp.zeros_like(q))
            parts = []
            o = jnp.zeros((tile, wide), F32)
            for c in range(0, keys, chunk):
                s = lax.dot_general(qh, k_ref[c : c + chunk, :], NT, preferred_element_type=F32)
                e = jnp.exp2(s * EXP2_SCALE)
                o += jnp.dot(e.astype(BF16), v_ref[c : c + chunk, :], preferred_element_type=F32)
                parts.append(e)
            inverse = 1.0 / o[:, part : part + 1]
            result = jnp.where((lane >= h * HEAD) & (lane < (h + 1) * HEAD), o * inverse, result)
            weight = inverse * weigh
            for c, e in zip(range(0, keys, chunk), parts):
                mass[:, c : c + chunk] += jnp.sum((e * weight).reshape(tile // 8, 8, chunk), axis=0)
        context[r, pl.ds(first, tile), :] = result[:, :part].astype(BF16)

        @pl.when(t == tiles - 1)
        def _():
            pl.semaphore_wait(barrier, seq_count - 1)

        @pl.when((t % tiles == tiles - 1) & (t < (GROUPS - 1) * tiles))
        def _():
            send_back(r).start()

        return carry

    lax.fori_loop(0, GROUPS * tiles, work, 0)
    masses[0, :, :keys] = jnp.sum(mass[...], axis=0, keepdims=True)
    masses[0, :, keys:] = count_ref[...]
    for p in range(1, seq_count):
        send_mass(p).start()

    def weights(r):
        return w_ref[pl.ds(pl.multiple_of((group + r) % GROUPS * part, part), part), :]

    total = middle_ref[...].astype(F32)
    total += jnp.dot(context[0], weights(0), preferred_element_type=F32)
    for r in range(1, GROUPS):
        send_back(r).wait()
        total += jnp.dot(landed[r], weights(r), preferred_element_type=F32)
    o_ref[...] = total.astype(BF16)
    for p in range(1, seq_count):
        send_mass(p).wait()
    mass_ref[...] = jnp.sum(masses[...], axis=0)


def cross_attend(seq_count, count, queries, pieces, middle, x_out):
    groups = len(queries)
    rows, wide = queries[0].shape
    keys = sum(piece.shape[0] for piece in pieces)
    part = wide - HEAD
    vmem = pl.BlockSpec(memory_space=pltpu.VMEM)
    return pl.pallas_call(
        functools.partial(cross_kernel, seq_count, 512, len(pieces)),
        out_shape=(
            jax.ShapeDtypeStruct(middle.shape, BF16),
            jax.ShapeDtypeStruct((1, keys + 128), F32),
        ),
        in_specs=[vmem] * (3 + groups + len(pieces)),
        out_specs=(vmem, vmem),
        scratch_shapes=[
            pltpu.VMEM((groups, rows, wide), BF16),
            pltpu.VMEM((keys, wide), BF16),
            pltpu.VMEM((keys, wide), BF16),
            pltpu.VMEM((groups, rows, part), BF16),
            pltpu.VMEM((groups, rows, part), BF16),
            pltpu.VMEM((8, keys), F32),
            pltpu.VMEM((seq_count, 1, keys + 128), F32),
            pltpu.SemaphoreType.DMA((groups,)),
            pltpu.SemaphoreType.DMA((groups,)),
            pltpu.SemaphoreType.DMA((seq_count,)),
            pltpu.SemaphoreType.DMA((seq_count,)),
        ],
        compiler_params=pltpu.CompilerParams(
            vmem_limit_bytes=48 * 1024 * 1024, collective_id=0, has_side_effects=True
        ),
        cost_estimate=pl.CostEstimate(
            flops=16 * groups * rows * keys * part,
            bytes_accessed=4 * keys * wide + 4 * rows * wide,
            transcendentals=3 * groups * rows * keys,
        ),
    )(count, middle, x_out, *queries, *pieces)


def local(
    hidden, token_ids, w_query, w_keyval, w_out, x_query, x_out, shortlist, code_row, code_cache
):
    doc_hidden = hidden[0]
    doc_tokens = token_ids[0]
    tok_rows, width = doc_hidden.shape
    seq_count = lax.axis_size("seq")
    doc_count = lax.axis_size("doc")
    devices = seq_count * doc_count
    across = seq_count // GROUPS
    seq_index = lax.axis_index("seq")
    doc_index = lax.axis_index("doc")
    me = doc_index * seq_count + seq_index
    group = seq_index // across
    cand_count = shortlist.shape[1]
    code_dev = code_cache.shape[0]
    capacity = 8 * cand_count // (5 * devices)
    slots = devices * capacity
    part = width // GROUPS

    up = [(i, i + 1) for i in range(seq_count - 1)]
    down = [(i + 1, i) for i in range(seq_count - 1)]
    live = (doc_tokens != 0).astype(F32)
    flagged = jnp.concatenate(
        [doc_hidden, jnp.broadcast_to(live.astype(BF16)[:, None], (tok_rows, 2 * HEAD))], axis=1
    )
    low = lax.ppermute(flagged[tok_rows - HALF_WIN :], "seq", up)
    high = lax.ppermute(flagged[:HALF_WIN], "seq", down)
    extended = jnp.concatenate([low, flagged, high])

    cache_rows = code_row[shortlist[0]]
    relative = [cache_rows]
    for r in range(1, doc_count):
        relative.append(
            lax.ppermute(cache_rows, "doc", [(i, (i + r) % doc_count) for i in range(doc_count)])
        )
    relative = jnp.stack(relative)
    docs = jnp.arange(doc_count, dtype=jnp.int32)
    source = (doc_index - docs) % doc_count
    rows_of = jnp.sum(
        jnp.where((source[None, :] == docs[:, None])[:, :, None], relative[None], 0), axis=1
    )
    order = jnp.arange(cand_count, dtype=jnp.int32)
    before = (order[:, None] < order[None, :]).astype(BF16)
    held = rows_of // code_dev == me
    rank = jnp.dot(held.astype(BF16), before, preferred_element_type=F32).astype(jnp.int32)
    slot = jnp.arange(capacity, dtype=jnp.int32)
    request = jnp.sum(
        jnp.where(
            held[:, None, :] & (rank[:, None, :] == slot[None, :, None]),
            (rows_of % code_dev)[:, None, :],
            0,
        ),
        axis=2,
    )
    picked = gather_rows(request.reshape(-1), code_cache, capacity, across)
    inner = DESC // across // CHUNKS
    arrived = []
    for chunk in picked:
        chunk = chunk.reshape(devices, inner * capacity, 2 * part)
        if arrived:
            chunk, arrived[-1] = lax.optimization_barrier((chunk, arrived[-1]))
        arrived.append(
            lax.all_to_all(chunk, ("doc", "seq"), split_axis=0, concat_axis=0, tiled=True)
        )

    owner = cache_rows // code_dev
    onehot = (owner[:, None] == jnp.arange(devices, dtype=jnp.int32)[None, :]).astype(BF16)
    ahead = jnp.dot(before.T, onehot, preferred_element_type=F32)
    slot_rank = jnp.sum(ahead * onehot, axis=1).astype(jnp.int32)
    slot_index = owner * capacity + slot_rank
    spot = jnp.arange(slots * inner, dtype=jnp.int32)
    spot_slot = spot // (inner * capacity) * capacity + spot % capacity
    descs = jnp.arange(inner, dtype=jnp.int32)
    choose = (slot_index[None, :, None] == spot_slot[None, None, :]) & (
        descs[:, None, None] == (spot // capacity % inner)[None, None, :]
    )
    choose = choose.astype(BF16).reshape(inner * cand_count, -1)

    normed = layer_norm(extended[:, :width].astype(F32)).astype(BF16)
    keyval = jnp.dot(normed, w_keyval, preferred_element_type=F32).astype(BF16)
    query = jnp.dot(
        normed[HALF_WIN : HALF_WIN + tok_rows], w_query, preferred_element_type=F32
    ).astype(BF16)
    valid = extended[:, width].astype(F32)[None]
    context = window_attend(valid, query, keyval)
    middle = (
        doc_hidden.astype(F32) + jnp.dot(context, w_out, preferred_element_type=F32)
    ).astype(BF16)
    middle_wide = middle.astype(F32)
    cross_normed = layer_norm(middle_wide).astype(BF16)
    wide = part + HEAD
    blank = jnp.zeros((width, HEAD), BF16)
    spread = []
    for g in range(GROUPS):
        spread += [blank, x_query[:, g * part : (g + 1) * part]]
    spread = jnp.concatenate(spread, axis=1)
    flag = (jnp.arange(GROUPS * wide) % wide < HEAD)[None, :]
    cross_query = jnp.dot(cross_normed, spread, preferred_element_type=F32)
    cross_query = jnp.where(flag, live[:, None], cross_query).astype(BF16)

    def turn(r):
        return [
            (i, (i // across + r) % GROUPS * across + i % across) for i in range(seq_count)
        ]

    def piece(array, g):
        return lax.dynamic_slice_in_dim(array, g * wide, wide, axis=1)

    queries = [piece(cross_query, group)]
    for r in range(1, GROUPS):
        queries.append(
            lax.ppermute(piece(cross_query, (group + r) % GROUPS), "seq", turn(r))
        )

    pieces = []
    for chunk in arrived:
        own_rows = jnp.dot(
            choose, chunk.reshape(-1, 2 * part), preferred_element_type=F32
        ).astype(BF16)
        pieces.append(own_rows)
        for r in range(1, across):
            step = [(i, i // across * across + (i % across + r) % across) for i in range(seq_count)]
            pieces.append(lax.ppermute(own_rows, "seq", step))

    count = jnp.full((1, 128), jnp.sum(live))
    refined, mass = cross_attend(
        seq_count, count, queries, pieces, middle, x_out
    )
    cand_mass = jnp.sum(mass[0, :-128].reshape(DESC, cand_count), axis=0)
    cand_score = cand_count * cand_mass / (HEADS * mass[0, -1])
    return (refined[None], cand_score[None])


def solution(mesh):
    return jax.shard_map(
        local,
        mesh=mesh,
        in_specs=(
            P("doc", "seq", None),
            P("doc", "seq"),
            P(),
            P(),
            P(),
            P(),
            P(),
            P("doc", None),
            P(),
            P(("doc", "seq"), None, None, None),
        ),
        out_specs=(P("doc", "seq", None), P("doc", None)),
        check_vma=False,
    )
```

```python
import functools
import math

import jax
import jax.numpy as jnp
from jax import lax
from jax.experimental import pallas as pl
from jax.experimental.pallas import tpu as pltpu
from jax.sharding import PartitionSpec as P

HEADS = 12
HEAD = 64
HALF_WIN = 256
DESC = 8
GROUPS = 4
CHUNKS = 1
EXP2_SCALE = math.log2(math.e) / math.sqrt(HEAD)
F32 = jnp.float32
BF16 = jnp.bfloat16
NT = (((1,), (1,)), ((), ()))


def layer_norm(values):
    centered = values - jnp.mean(values, axis=-1, keepdims=True)
    spread = jnp.mean(centered * centered, axis=-1, keepdims=True)
    return centered * lax.rsqrt(spread + 1e-05)


def window_kernel(valid_ref, q_ref, k_ref, v_ref, o_ref, bias):
    rows = q_ref.shape[0]
    half = HALF_WIN
    blocks = rows // half
    width = 3 * half

    @pl.when(pl.program_id(0) == 0)
    def _():
        for b in range(blocks):
            i = lax.broadcasted_iota(jnp.int32, (half, width), 0)
            j = lax.broadcasted_iota(jnp.int32, (half, width), 1)
            ok = valid_ref[:, b * half : b * half + width] > 0.0
            allowed = (j >= i) & (j <= i + 2 * half) & (ok | (j == i + half))
            bias[b] = jnp.where(allowed, 0.0, -1e30)

    k = k_ref[...]
    v = v_ref[...]
    v = jnp.concatenate([v, jnp.ones_like(v)], axis=1)
    lane = lax.broadcasted_iota(jnp.int32, (half, 2 * HEAD), 1)
    for b in range(blocks):
        q = q_ref[b * half : (b + 1) * half, :]
        kb = k[b * half : b * half + width]
        vb = v[b * half : b * half + width]
        outs = []
        for h in range(2):
            mine = (lane >= h * HEAD) & (lane < (h + 1) * HEAD)
            s = lax.dot_general(
                jnp.where(mine, q, jnp.zeros_like(q)), kb, NT, preferred_element_type=F32
            )
            e = jnp.exp2(s * EXP2_SCALE + bias[b])
            o = jnp.dot(e.astype(BF16), vb, preferred_element_type=F32)
            outs.append(o[:, : 2 * HEAD] / o[:, 2 * HEAD :])
        o_ref[b * half : (b + 1) * half, :] = jnp.where(lane < HEAD, outs[0], outs[1]).astype(BF16)


def window_attend(valid, query, keyval):
    rows, width = query.shape
    pairs = width // (2 * HEAD)
    span = rows + 2 * HALF_WIN

    def cols(r, first):
        return pl.BlockSpec((r, 2 * HEAD), lambda p: (0, p + first))

    return pl.pallas_call(
        window_kernel,
        grid=(pairs,),
        out_shape=jax.ShapeDtypeStruct((rows, width), BF16),
        in_specs=[
            pl.BlockSpec((1, span), lambda p: (0, 0)),
            cols(rows, 0),
            cols(span, 0),
            cols(span, pairs),
        ],
        out_specs=cols(rows, 0),
        scratch_shapes=[pltpu.VMEM((rows // HALF_WIN, HALF_WIN, 3 * HALF_WIN), F32)],
        compiler_params=pltpu.CompilerParams(vmem_limit_bytes=48 * 1024 * 1024),
        cost_estimate=pl.CostEstimate(
            flops=8 * rows * 3 * HALF_WIN * width,
            bytes_accessed=8 * rows * width,
            transcendentals=rows * 3 * HALF_WIN * HEADS,
        ),
    )(valid, query, keyval, keyval)


def gather_kernel(docs, capacity, request_ref, cache_ref, order_ref, *refs):
    *outs, held, sems = refs
    count = docs * capacity
    step = 2 * DESC
    part = outs[0].shape[-1] // 2

    def fetch(i):
        row = pl.multiple_of(request_ref[i] * step, step)
        return pltpu.make_async_copy(
            cache_ref.at[pl.ds(row, step)], held.at[pl.ds(i * step, step)], sems.at[i]
        )

    for i in range(count):
        fetch(i).start()
    rows = capacity * step
    half = capacity * DESC
    for d in range(docs):
        for i in range(d * capacity, (d + 1) * capacity):
            fetch(i).wait()
        ordered = jnp.dot(
            order_ref[...], held[d * rows : (d + 1) * rows, :], preferred_element_type=F32
        ).astype(BF16)
        for g in range(GROUPS):
            cols = slice(g * part, (g + 1) * part)
            both = jnp.concatenate([ordered[:half, cols], ordered[half:, cols]], axis=1)
            size = half // len(outs)
            for c, out_ref in enumerate(outs):
                out_ref[d, g] = both[c * size : (c + 1) * size]


def gather_rows(request, cache, capacity, across):
    docs = request.shape[0] // capacity
    codes, pair, desc, width = cache.shape
    part = width // GROUPS
    rows = capacity * pair * desc
    out = jnp.arange(rows)
    inner = desc // across // CHUNKS
    chunk = out // (desc * capacity // CHUNKS) % CHUNKS
    column = out // (inner * capacity) % across
    position = (column * CHUNKS + chunk) * inner + out // capacity % inner
    source = out % capacity * (2 * desc) + (1 - out // (desc * capacity)) * desc + position
    order = (source[:, None] == out[None, :]).astype(BF16)
    return pl.pallas_call(
        functools.partial(gather_kernel, docs, capacity),
        out_shape=[jax.ShapeDtypeStruct((docs, GROUPS, rows // 2 // CHUNKS, 2 * part), BF16)]
        * CHUNKS,
        in_specs=[
            pl.BlockSpec(memory_space=pltpu.SMEM),
            pl.BlockSpec(memory_space=pl.ANY),
            pl.BlockSpec(memory_space=pltpu.VMEM),
        ],
        out_specs=[pl.BlockSpec(memory_space=pltpu.VMEM)] * CHUNKS,
        scratch_shapes=[
            pltpu.VMEM((docs * rows, width), BF16),
            pltpu.SemaphoreType.DMA((docs * capacity,)),
        ],
        compiler_params=pltpu.CompilerParams(vmem_limit_bytes=48 * 1024 * 1024),
        cost_estimate=pl.CostEstimate(
            flops=2 * docs * rows * rows * width,
            bytes_accessed=4 * docs * rows * width,
            transcendentals=0,
        ),
    )(request, cache.reshape(codes * pair * desc, width), order)


def cross_kernel(
    seq_count,
    chunk,
    count_ref,
    middle_ref,
    w_ref,
    *refs,
):
    queries, refs = refs[:GROUPS], refs[GROUPS:]
    own_ref, o_ref, mass_ref, q_ref, k_ref, v_ref, context, landed, mass, masses = refs[:10]
    others, held, partial, send_sem, recv_sem, mass_send, mass_recv, row_send, row_recv = refs[10:]
    me = lax.axis_index("seq")
    across = seq_count // GROUPS
    group = me // across
    column = me % across
    keys, wide = k_ref.shape
    tile = 256
    tiles = q_ref.shape[1] // tile
    part = wide - HEAD
    heads = part // HEAD
    lane = lax.broadcasted_iota(jnp.int32, (tile, wide), 1)

    barrier = pltpu.get_barrier_semaphore()
    for p in range(1, seq_count):
        pl.semaphore_signal(
            barrier,
            inc=1,
            device_id={"seq": (me + p) % seq_count},
            device_id_type=pl.DeviceIdType.MESH,
        )
    mass[...] = jnp.zeros_like(mass)
    size = own_ref.shape[0]

    def send_rows(p):
        return pltpu.make_async_remote_copy(
            src_ref=own_ref,
            dst_ref=others.at[p - 1],
            send_sem=row_send.at[p],
            recv_sem=row_recv.at[p],
            device_id={"seq": group * across + (column + p) % across},
            device_id_type=pl.DeviceIdType.MESH,
        )

    def place(n, piece):
        k_ref[n * size : (n + 1) * size, :] = piece[:, part - HEAD :]
        ahead = lax.broadcasted_iota(jnp.int32, (size, wide), 1) < part
        v_ref[n * size : (n + 1) * size, :] = jnp.where(ahead, piece[:, :wide], jnp.ones((), BF16))

    def cuts(start, stop):
        return [(c, min(c + chunk, stop)) for c in range(start, stop, chunk)]

    pl.semaphore_wait(barrier, seq_count - 1)
    for p in range(1, across):
        send_rows(p).start()
    place(0, own_ref[...])
    for r, query in enumerate(queries):
        q_ref[r] = query[...]

    def send_back(r):
        return pltpu.make_async_remote_copy(
            src_ref=context.at[r],
            dst_ref=landed.at[r],
            send_sem=send_sem.at[r],
            recv_sem=recv_sem.at[r],
            device_id={"seq": (group + GROUPS - r) % GROUPS * across + column},
            device_id_type=pl.DeviceIdType.MESH,
        )

    def send_mass(p):
        return pltpu.make_async_remote_copy(
            src_ref=masses.at[0],
            dst_ref=masses.at[p],
            send_sem=mass_send.at[p],
            recv_sem=mass_recv.at[p],
            device_id={"seq": (me + p) % seq_count},
            device_id_type=pl.DeviceIdType.MESH,
        )

    def tile_queries(t):
        r = (t // tiles + 1) % GROUPS
        first = pl.multiple_of(t % tiles * tile, tile)
        return r, first, q_ref[r, pl.ds(first, tile), :]

    def scored(q, h, c, d):
        mine = (lane >= (h + 1) * HEAD) & (lane < (h + 2) * HEAD)
        qh = jnp.where(mine, q, jnp.zeros_like(q))
        s = lax.dot_general(qh, k_ref[c:d, :], NT, preferred_element_type=F32)
        e = jnp.exp2(s * EXP2_SCALE)
        eb = e.astype(BF16)
        return e, eb, jnp.dot(eb, v_ref[c:d, :], preferred_element_type=F32)

    def own_work(t, carry):
        r, first, q = tile_queries(t)
        result = jnp.zeros((tile, wide), F32)
        for h in range(heads):
            o = jnp.zeros((tile, wide), F32)
            for c, d in cuts(0, size):
                e, eb, more = scored(q, h, c, d)
                held[t, h, :, c:d] = eb
                o += more
            kept = ((lane >= h * HEAD) & (lane < (h + 1) * HEAD)) | (lane == part + h)
            result = jnp.where(kept, o, result)
        partial[t] = result
        return carry

    lax.fori_loop(0, GROUPS * tiles, own_work, 0)
    for p in range(1, across):
        send_rows(p).wait()
        place(p, others[p - 1])

    def work(t, carry):
        r, first, q = tile_queries(t)
        weigh = q[:, 0:1].astype(F32)
        before = partial[t]
        result = jnp.zeros((tile, wide), F32)
        for h in range(heads):
            o = before
            parts = []
            for c, d in cuts(size, keys):
                e, eb, more = scored(q, h, c, d)
                o += more
                parts.append(e)
            inverse = 1.0 / o[:, part + h : part + h + 1]
            result = jnp.where((lane >= h * HEAD) & (lane < (h + 1) * HEAD), o * inverse, result)
            weight = inverse * weigh
            for c, d in cuts(0, size):
                share = held[t, h, :, c:d].astype(F32) * weight
                mass[:, c:d] += jnp.sum(share.reshape(tile // 8, 8, d - c), axis=0)
            for (c, d), e in zip(cuts(size, keys), parts):
                mass[:, c:d] += jnp.sum((e * weight).reshape(tile // 8, 8, d - c), axis=0)
        context[r, pl.ds(first, tile), :] = result[:, :part].astype(BF16)

        @pl.when((t % tiles == tiles - 1) & (t < (GROUPS - 1) * tiles))
        def _():
            send_back(r).start()

        return carry

    lax.fori_loop(0, GROUPS * tiles, work, 0)
    masses[0, :, :keys] = jnp.sum(mass[...], axis=0, keepdims=True)
    masses[0, :, keys:] = count_ref[...]
    for p in range(1, seq_count):
        send_mass(p).start()

    def weights(r):
        return w_ref[pl.ds(pl.multiple_of((group + r) % GROUPS * part, part), part), :]

    total = middle_ref[...].astype(F32)
    total += jnp.dot(context[0], weights(0), preferred_element_type=F32)
    for r in range(1, GROUPS):
        send_back(r).wait()
        total += jnp.dot(landed[r], weights(r), preferred_element_type=F32)
    o_ref[...] = total.astype(BF16)
    for p in range(1, seq_count):
        send_mass(p).wait()
    mass_ref[...] = jnp.sum(masses[...], axis=0)


def cross_attend(seq_count, count, queries, own_rows, middle, x_out):
    groups = len(queries)
    rows, wide = queries[0].shape
    across = seq_count // groups
    size = own_rows.shape[0]
    keys = across * size
    tiles = groups * rows // 256
    part = wide - HEAD
    vmem = pl.BlockSpec(memory_space=pltpu.VMEM)
    return pl.pallas_call(
        functools.partial(cross_kernel, seq_count, 512),
        out_shape=(
            jax.ShapeDtypeStruct(middle.shape, BF16),
            jax.ShapeDtypeStruct((1, keys + 128), F32),
        ),
        in_specs=[vmem] * (4 + groups),
        out_specs=(vmem, vmem),
        scratch_shapes=[
            pltpu.VMEM((groups, rows, wide), BF16),
            pltpu.VMEM((keys, wide), BF16),
            pltpu.VMEM((keys, wide), BF16),
            pltpu.VMEM((groups, rows, part), BF16),
            pltpu.VMEM((groups, rows, part), BF16),
            pltpu.VMEM((8, keys), F32),
            pltpu.VMEM((seq_count, 1, keys + 128), F32),
            pltpu.VMEM((max(across - 1, 1), size, own_rows.shape[1]), BF16),
            pltpu.VMEM((tiles, (wide - HEAD) // HEAD, 256, size), BF16),
            pltpu.VMEM((tiles, 256, wide), F32),
            pltpu.SemaphoreType.DMA((groups,)),
            pltpu.SemaphoreType.DMA((groups,)),
            pltpu.SemaphoreType.DMA((seq_count,)),
            pltpu.SemaphoreType.DMA((seq_count,)),
            pltpu.SemaphoreType.DMA((across,)),
            pltpu.SemaphoreType.DMA((across,)),
        ],
        compiler_params=pltpu.CompilerParams(
            vmem_limit_bytes=56 * 1024 * 1024, collective_id=0, has_side_effects=True
        ),
        cost_estimate=pl.CostEstimate(
            flops=16 * groups * rows * keys * part,
            bytes_accessed=4 * keys * wide + 4 * rows * wide,
            transcendentals=3 * groups * rows * keys,
        ),
    )(count, middle, x_out, *queries, own_rows)


def local(
    hidden, token_ids, w_query, w_keyval, w_out, x_query, x_out, shortlist, code_row, code_cache
):
    doc_hidden = hidden[0]
    doc_tokens = token_ids[0]
    tok_rows, width = doc_hidden.shape
    seq_count = lax.axis_size("seq")
    doc_count = lax.axis_size("doc")
    devices = seq_count * doc_count
    across = seq_count // GROUPS
    seq_index = lax.axis_index("seq")
    doc_index = lax.axis_index("doc")
    me = doc_index * seq_count + seq_index
    group = seq_index // across
    cand_count = shortlist.shape[1]
    code_dev = code_cache.shape[0]
    capacity = 8 * cand_count // (5 * devices)
    slots = devices * capacity
    part = width // GROUPS

    up = [(i, i + 1) for i in range(seq_count - 1)]
    down = [(i + 1, i) for i in range(seq_count - 1)]
    live = (doc_tokens != 0).astype(F32)
    flagged = jnp.concatenate(
        [doc_hidden, jnp.broadcast_to(live.astype(BF16)[:, None], (tok_rows, 2 * HEAD))], axis=1
    )
    low = lax.ppermute(flagged[tok_rows - HALF_WIN :], "seq", up)
    high = lax.ppermute(flagged[:HALF_WIN], "seq", down)
    extended = jnp.concatenate([low, flagged, high])

    cache_rows = code_row[shortlist[0]]
    relative = [cache_rows]
    for r in range(1, doc_count):
        relative.append(
            lax.ppermute(cache_rows, "doc", [(i, (i + r) % doc_count) for i in range(doc_count)])
        )
    relative = jnp.stack(relative)
    docs = jnp.arange(doc_count, dtype=jnp.int32)
    source = (doc_index - docs) % doc_count
    rows_of = jnp.sum(
        jnp.where((source[None, :] == docs[:, None])[:, :, None], relative[None], 0), axis=1
    )
    order = jnp.arange(cand_count, dtype=jnp.int32)
    before = (order[:, None] < order[None, :]).astype(BF16)
    held = rows_of // code_dev == me
    rank = jnp.dot(held.astype(BF16), before, preferred_element_type=F32).astype(jnp.int32)
    slot = jnp.arange(capacity, dtype=jnp.int32)
    request = jnp.sum(
        jnp.where(
            held[:, None, :] & (rank[:, None, :] == slot[None, :, None]),
            (rows_of % code_dev)[:, None, :],
            0,
        ),
        axis=2,
    )
    picked = gather_rows(request.reshape(-1), code_cache, capacity, across)
    inner = DESC // across // CHUNKS
    arrived = []
    for chunk in picked:
        chunk = chunk.reshape(devices, inner * capacity, 2 * part)
        if arrived:
            chunk, arrived[-1] = lax.optimization_barrier((chunk, arrived[-1]))
        arrived.append(
            lax.all_to_all(chunk, ("doc", "seq"), split_axis=0, concat_axis=0, tiled=True)
        )

    owner = cache_rows // code_dev
    onehot = (owner[:, None] == jnp.arange(devices, dtype=jnp.int32)[None, :]).astype(BF16)
    ahead = jnp.dot(before.T, onehot, preferred_element_type=F32)
    slot_rank = jnp.sum(ahead * onehot, axis=1).astype(jnp.int32)
    slot_index = owner * capacity + slot_rank
    spot = jnp.arange(slots * inner, dtype=jnp.int32)
    spot_slot = spot // (inner * capacity) * capacity + spot % capacity
    descs = jnp.arange(inner, dtype=jnp.int32)
    choose = (slot_index[None, :, None] == spot_slot[None, None, :]) & (
        descs[:, None, None] == (spot // capacity % inner)[None, None, :]
    )
    choose = choose.astype(BF16).reshape(inner * cand_count, -1)

    normed = layer_norm(extended[:, :width].astype(F32)).astype(BF16)
    keyval = jnp.dot(normed, w_keyval, preferred_element_type=F32).astype(BF16)
    query = jnp.dot(
        normed[HALF_WIN : HALF_WIN + tok_rows], w_query, preferred_element_type=F32
    ).astype(BF16)
    valid = extended[:, width].astype(F32)[None]
    context = window_attend(valid, query, keyval)
    middle = (
        doc_hidden.astype(F32) + jnp.dot(context, w_out, preferred_element_type=F32)
    ).astype(BF16)
    middle_wide = middle.astype(F32)
    cross_normed = layer_norm(middle_wide).astype(BF16)
    wide = part + HEAD
    blank = jnp.zeros((width, HEAD), BF16)
    spread = []
    for g in range(GROUPS):
        spread += [blank, x_query[:, g * part : (g + 1) * part]]
    spread = jnp.concatenate(spread, axis=1)
    flag = (jnp.arange(GROUPS * wide) % wide < HEAD)[None, :]
    cross_query = jnp.dot(cross_normed, spread, preferred_element_type=F32)
    cross_query = jnp.where(flag, live[:, None], cross_query).astype(BF16)

    def turn(r):
        return [
            (i, (i // across + r) % GROUPS * across + i % across) for i in range(seq_count)
        ]

    def piece(array, g):
        return lax.dynamic_slice_in_dim(array, g * wide, wide, axis=1)

    queries = [piece(cross_query, group)]
    for r in range(1, GROUPS):
        queries.append(
            lax.ppermute(piece(cross_query, (group + r) % GROUPS), "seq", turn(r))
        )

    own_rows = jnp.dot(
        choose, arrived[0].reshape(-1, 2 * part), preferred_element_type=F32
    ).astype(BF16)
    count = jnp.full((1, 128), jnp.sum(live))
    refined, mass = cross_attend(
        seq_count, count, queries, own_rows, middle, x_out
    )
    cand_mass = jnp.sum(mass[0, :-128].reshape(DESC, cand_count), axis=0)
    cand_score = cand_count * cand_mass / (HEADS * mass[0, -1])
    return (refined[None], cand_score[None])


def solution(mesh):
    return jax.shard_map(
        local,
        mesh=mesh,
        in_specs=(
            P("doc", "seq", None),
            P("doc", "seq"),
            P(),
            P(),
            P(),
            P(),
            P(),
            P("doc", None),
            P(),
            P(("doc", "seq"), None, None, None),
        ),
        out_specs=(P("doc", "seq", None), P("doc", None)),
        check_vma=False,
    )
```
